512 devices in a mesh: dom: 64 (over z, x, core), band: 8 (over y).
Axes of the slice: x: 4, y: 8, z: 8, core: 2. Of those that a mesh axis runs over, the one named last changes fastest.
Arguments:
- orbitals: float32 [256, 64, 6, 512], P('band', 'dom'), may hold values from -6 to 6
- potential: float32 [64, 6, 512], P('dom'), may hold values from -1 to 1
- proj_shape: float32 [64, 64, 6, 512], P(None, 'dom'), may hold values from -4 to 4
- proj_strength: float32 [64], replicated, may hold values from -6 to -2
- atom_z: int32 [64], replicated, may hold values from 0 to 38
- atom_x: int32 [64], replicated, may hold values from 0 to 54
- atom_y: int32 [64], replicated, may hold values from 0 to 54
Outputs:
- rotated: float32 [256, 64, 6, 512], P('band', 'dom')
- projected: float32 [256, 256], P('band')
The draws below stay inside these ranges and needn't reach their ends.
All inputs are finite; a program needn't handle non-finite values.
Results may differ from the reference program's by a relative error of at most 0.0003.
Values sent between devices are 32-bit elements; how exact they have to be, the bound alone decides.
No kernel may reach another device: no remote copies, remote signals or barrier semaphores. Data moves between devices by JAX's collectives and lax.ppermute only.
A program may use at most 64 MiB of HBM per device.

```python
import jax
import jax.numpy as jnp
from jax import lax

NB = 256
XBLOCKS = 8
CX = 8
NY = 64
CZ = 6
NPJ = 64
DEGREE = 4
SPAN = 10
NPEN = 64
NZ = 48
NX = 64
CXY = 512
PROJ_CELLS = 1000
NCELLS = 196608


def place_ends(entries, key, smallest, top_value):
    spot = [jax.random.randint(jax.random.fold_in(key, axis), (), 0, length) for axis, length in enumerate(entries.shape)]
    longest = entries.shape.index(max(entries.shape))
    next_to = spot[:longest] + [(spot[longest] + 1) % entries.shape[longest]] + spot[longest + 1:]
    return entries.at[tuple(spot)].set(smallest).at[tuple(next_to)].set(top_value)


def levels(own_key, shape, shards, least, largest):
    level, own = 1.0, jax.random.fold_in(own_key, 6)
    for axis_at, blocks in shards:
        steps = jnp.exp(jax.random.uniform(jax.random.fold_in(own, axis_at), (blocks,), jnp.float32, least / len(shards), largest / len(shards)))
        level = level * jnp.repeat(steps, shape[axis_at] // blocks).reshape([-1 if axis == axis_at else 1 for axis in range(len(shape))])
    return level


def scatter_about(key, dims, spread, limit, shards=(), kind=jnp.bfloat16):
    values = jax.random.normal(key, dims, jnp.float32) * spread
    if len(shards) > 0:
        values = levels(key, dims, shards, -0.22, 0.18) * values
    return jnp.clip(values, min=-limit, max=limit).astype(kind)


def setup_inputs(seed: int = 0) -> dict:
    streams_of = jax.random.split(jax.random.key(seed), 8)
    orbitals = scatter_about(streams_of[0], (NB, NPEN, CZ, CXY), 1.0, 6.0, ((0, 8), (1, 64)), jnp.float32)
    potential = jnp.clip(jax.random.uniform(streams_of[1], (NPEN, CZ, CXY), jnp.float32, -1.0, 1.0) * levels(streams_of[1], (NPEN, CZ, CXY), ((0, 64),), -0.4, 0.0), -1.0, 1.0)
    proj_shape = scatter_about(streams_of[2], (NPJ, NPEN, CZ, CXY), 1.0, 4.0, ((1, 64),), jnp.float32)
    proj_strength = jnp.clip(jax.random.uniform(streams_of[3], (NPJ,), jnp.float32, -6.0, -2.0), -6.0, -2.0)
    atom_z = place_ends(jax.random.randint(streams_of[4], (NPJ,), 0, NZ - SPAN + 1), jax.random.fold_in(streams_of[4], 1), 0, NZ - SPAN).astype(jnp.int32)
    atom_x = place_ends(jax.random.randint(streams_of[5], (NPJ,), 0, NX - SPAN + 1), jax.random.fold_in(streams_of[5], 1), 0, NX - SPAN).astype(jnp.int32)
    atom_y = place_ends(jax.random.randint(streams_of[6], (NPJ,), 0, NY - SPAN + 1), jax.random.fold_in(streams_of[6], 1), 0, NY - SPAN).astype(jnp.int32)
    return dict(orbitals=orbitals, potential=potential, proj_shape=proj_shape, proj_strength=proj_strength, atom_z=atom_z, atom_x=atom_x, atom_y=atom_y)


COEFFS = [-5369.0 / 1800.0, 12.0 / 7.0, -15.0 / 56.0, 10.0 / 189.0, -1.0 / 112.0, 2.0 / 1925.0, -1.0 / 16632.0]
CENTER_VALUE = 9.5
HALF_WIDTH = 6.5

def to_grid(array):
    leading = array.shape[0]
    shaped = array.reshape(leading, NZ // CZ, XBLOCKS, CZ, CX, NY)
    return jnp.transpose(shaped, (0, 1, 3, 2, 4, 5)).reshape(leading, NZ, NX, NY)

def from_grid(array):
    leading = array.shape[0]
    shaped = array.reshape(leading, NZ // CZ, CZ, XBLOCKS, CX, NY)
    return jnp.transpose(shaped, (0, 1, 3, 2, 4, 5)).reshape(leading, NZ // CZ * XBLOCKS, CZ, CX * NY)

def local_part(values, potential):
    padded = jnp.pad(values, ((0, 0), (6, 6), (6, 6), (6, 6)))
    summed = 3.0 * COEFFS[0] * values
    for offset in range(1, 7):
        along_z = padded[:, 6 + offset:6 + offset + NZ, 6:6 + NX, 6:6 + NY] + padded[:, 6 - offset:6 - offset + NZ, 6:6 + NX, 6:6 + NY]
        along_x = padded[:, 6:6 + NZ, 6 + offset:6 + offset + NX, 6:6 + NY] + padded[:, 6:6 + NZ, 6 - offset:6 - offset + NX, 6:6 + NY]
        along_y = padded[:, 6:6 + NZ, 6:6 + NX, 6 + offset:6 + offset + NY] + padded[:, 6:6 + NZ, 6:6 + NX, 6 - offset:6 - offset + NY]
        summed = summed + COEFFS[offset] * (along_z + along_x + along_y)
    return -0.5 * summed + potential[None] * values

def hamiltonian_apply(values, potential, projector, scaled_strength):
    result = local_part(values, potential)
    correlations = jnp.einsum('azxy,bzxy->ab', projector, values, precision=lax.Precision.HIGHEST)
    return result + jnp.einsum('ab,azxy->bzxy', correlations * scaled_strength[:, None], projector, precision=lax.Precision.HIGHEST)

def reference(orbitals, potential, proj_shape, proj_strength, atom_z, atom_x, atom_y):
    field_potential = to_grid(potential[None])[0]
    shapes = to_grid(proj_shape)
    z_cell = jnp.arange(NZ).astype(jnp.int32)
    x_cell = jnp.arange(NX).astype(jnp.int32)
    y_cell = jnp.arange(NY).astype(jnp.int32)
    in_z = (z_cell[None, :] >= atom_z[:, None]) & (z_cell[None, :] < atom_z[:, None] + SPAN)
    in_x = (x_cell[None, :] >= atom_x[:, None]) & (x_cell[None, :] < atom_x[:, None] + SPAN)
    in_y = (y_cell[None, :] >= atom_y[:, None]) & (y_cell[None, :] < atom_y[:, None] + SPAN)
    inside = in_z[:, :, None, None] & in_x[:, None, :, None] & in_y[:, None, None, :]
    projector = jnp.where(inside, shapes, 0.0)
    scaled_strength = proj_strength / PROJ_CELLS
    previous = to_grid(orbitals)
    current = (hamiltonian_apply(previous, field_potential, projector, scaled_strength) - CENTER_VALUE * previous) / HALF_WIDTH
    for repeat in range(DEGREE - 1):
        following = 2.0 * (hamiltonian_apply(current, field_potential, projector, scaled_strength) - CENTER_VALUE * current) / HALF_WIDTH - previous
        previous = current
        current = following
    filtered = current
    image = hamiltonian_apply(filtered, field_potential, projector, scaled_strength)
    flat_filtered = filtered.reshape(NB, NCELLS)
    flat_image = image.reshape(NB, NCELLS)
    hamiltonian = jnp.dot(flat_filtered, flat_image.T, precision=lax.Precision.HIGHEST) / NCELLS
    correlation = jnp.dot(flat_filtered, flat_filtered.T, precision=lax.Precision.HIGHEST) / NCELLS
    lower_factor = jnp.linalg.cholesky(correlation)
    identity = jnp.eye(NB, dtype=jnp.float32)
    inverse = lax.linalg.triangular_solve(lower_factor, identity, left_side=True, lower=True)
    projected = jnp.dot(jnp.dot(inverse, hamiltonian, precision=lax.Precision.HIGHEST), inverse.T, precision=lax.Precision.HIGHEST)
    rotated_flat = jnp.dot(inverse, flat_filtered, precision=lax.Precision.HIGHEST)
    rotated = from_grid(rotated_flat.reshape(NB, NZ, NX, NY))
    return (rotated, projected)
```

```python
import jax
import jax.numpy as jnp
import numpy as np
from jax import lax
from jax.experimental import pallas as pl
from jax.experimental.pallas import tpu as pltpu
from jax.sharding import PartitionSpec as P

NY = 64
NCELLS = 196608
PROJ_CELLS = 1000
COEFFS = [
    -5369.0 / 1800.0,
    12.0 / 7.0,
    -15.0 / 56.0,
    10.0 / 189.0,
    -1.0 / 112.0,
    2.0 / 1925.0,
    -1.0 / 16632.0,
]
CENTER = 9.5
HALF = 6.5
KIN = [-0.5 * c for c in COEFFS]
HIGH = lax.Precision.HIGHEST
F32 = jnp.float32


PIECE = 6
P1_ROWS = 40
BOX = 10
P2_ROWS = 48


def vmem():
    return pl.BlockSpec(memory_space=pltpu.VMEM)


def smem():
    return pl.BlockSpec(memory_space=pltpu.SMEM)


def params():
    return pltpu.CompilerParams(vmem_limit_bytes=56 * 1024 * 1024)


def pack_kernel(at_ref, pos_ref, proj_ref, pot_ref, out_ref, pad_ref):
    pad_ref[...] = jnp.zeros_like(pad_ref)
    pad_ref[:, 0:24, :] = proj_ref[...]
    lane = lax.broadcasted_iota(jnp.int32, (8, 128), 1)
    sub = lax.broadcasted_iota(jnp.int32, (8, 128), 0)
    z_cell = pos_ref[0] + sub
    x_first = pos_ref[1] + lane // 64
    slot = (lane % 64) // 16
    in_y = lane % 16 < 10

    def pair(i, carry):
        for m in range(2):
            a = 2 * i + m
            z0 = at_ref[0, a]
            x0 = at_ref[1, a]
            y0 = at_ref[2, a]
            in_z = (z_cell >= z0) & (z_cell < z0 + 10)
            packed = jnp.zeros((8, 128), F32)
            for j in range(4):
                x_cell = x_first + 2 * j
                inside = in_z & (x_cell >= x0) & (x_cell < x0 + 10)
                rows = pad_ref[a, pl.ds(j, 8, stride=4), :]
                rows = jnp.where(inside, rows, 0.0)
                rows = pltpu.roll(rows, (128 + 16 * j - y0) % 128, 1)
                packed = packed + jnp.where(in_y & (slot == j), rows, 0.0)
            out_ref[i, pl.ds(PIECE * m, PIECE), :] = packed[0:PIECE]
        out_ref[i, pl.ds(12, 24), :] = pot_ref[...]
        return carry

    lax.fori_loop(0, 32, pair, 0)


def boxes_kernel(at_ref, pos_ref, got_ref, orb_ref, out_ref, col_ref):
    col_ref[...] = jnp.zeros_like(col_ref)
    sub = lax.broadcasted_iota(jnp.int32, (16, 128), 0)
    for m in range(2):
        for zb in range(8):
            part = got_ref[4 * zb, PIECE * m : PIECE * (m + 1), :]
            for q in range(1, 4):
                part = part + got_ref[4 * zb + q, PIECE * m : PIECE * (m + 1), :]
            col_ref[m, 6 * zb : 6 * zb + 6, :] = part
    boxes = []
    for m in range(2):
        z0 = at_ref[0, 2 * pos_ref[2] + m]
        boxes.append(col_ref[m, pl.ds(z0, 16), :][0:BOX])

    def send(n, carry):
        out_ref[n, 0:BOX, :] = boxes[0]
        out_ref[n, BOX : 2 * BOX, :] = boxes[1]
        out_ref[n, 20:44, :] = orb_ref[n]
        out_ref[n, 44:48, :] = jnp.zeros((4, 128), F32)
        return carry

    lax.fori_loop(0, 32, send, 0)


def filter_kernel(
    at_ref, pos_ref, strength_ref, taps_ref, own_ref, oth_ref, ownp_ref, othp_ref, out_ref,
    fld, pot, tiles, parts, scaled,
):
    core = pos_ref[3]
    fld[...] = jnp.zeros_like(fld)
    tiles[...] = jnp.zeros_like(tiles)
    for src, src_pot, c in ((own_ref, ownp_ref, core), (oth_ref, othp_ref, 1 - core)):
        for i in range(32):
            zb, q = i // 4, i % 4
            for j in range(4):
                xp = 8 * q + 4 * c + j
                fld[0, 3 + xp, 8 + 6 * zb : 14 + 6 * zb, :] = src.at[i][pl.ds(20 + j, 6, stride=4), :]
                pot[xp, 6 * zb : 6 * zb + 6, :] = src_pot.at[i][pl.ds(12 + j, 6, stride=4), :]

    lane = lax.broadcasted_iota(jnp.int32, (BOX, 128), 1)
    slot = (lane % 64) // 16

    def expand(a, carry):
        xs = jnp.minimum(at_ref[1, a] // 2, 26)
        y0 = at_ref[2, a]
        start = BOX * (a % 2)
        own = own_ref[a // 2, pl.ds(start, BOX), :]
        oth = oth_ref[a // 2, pl.ds(start, BOX), :]
        for w in range(6):
            xp = xs + w
            j = xp % 4
            box = jnp.where((xp // 4) % 2 == core, own, oth)
            box = jnp.where(slot == j, box, 0.0)
            tiles[6 * a + w, 0:BOX, :] = pltpu.roll(box, (128 + y0 - 16 * j) % 128, 1)
        return carry

    lax.fori_loop(0, 64, expand, 0)

    ones = jnp.ones((128, 128), F32)
    low_half = lax.broadcasted_iota(jnp.int32, (48, 128), 1) < 64

    def step(cur, nxt, prev, ca, cb, cg):
        def inner(a, carry):
            xs = jnp.minimum(at_ref[1, a] // 2, 26)
            z0 = at_ref[0, a]
            win = fld[cur, pl.ds(3 + xs, 6), pl.ds(8 + z0, 16), :]
            prod = jnp.sum(win * tiles[pl.ds(6 * a, 6)], axis=0)
            parts[pl.ds(a, 1), :] = jnp.sum(prod, axis=0, keepdims=True)
            return carry

        lax.fori_loop(0, 64, inner, 0, unroll=4)
        sums = jnp.dot(parts[...], ones, precision=HIGH, preferred_element_type=F32)
        scaled[...] = sums * (ca * strength_ref[...])

        def along_y(t, carry):
            rows = fld[cur, pl.ds(3 + 8 * t, 8), 8:56, :].reshape(384, 128)
            got = jnp.dot(rows, taps_ref[...], precision=HIGH, preferred_element_type=F32)
            fld[nxt, pl.ds(3 + 8 * t, 8), 8:56, :] = got.reshape(8, 48, 128)
            return carry

        lax.fori_loop(0, 4, along_y, 0)

        def odd(x):
            def at(d):
                return fld[cur, 3 + x + d, 8:56, :]

            total = KIN[1] * (at(0) + at(-1)) + KIN[3] * (at(1) + at(-2)) + KIN[5] * (at(2) + at(-3))
            return pltpu.roll(total, 64, 1)

        def local(x, here):
            after = odd(x + 1)
            center = fld[cur, 3 + x, 8:56, :]
            total = fld[nxt, 3 + x, 8:56, :] + jnp.where(low_half, here, after)
            total = total + (3.0 * KIN[0] + pot[x]) * center
            for o in range(1, 7):
                pair = fld[cur, 3 + x, 8 + o : 56 + o, :] + fld[cur, 3 + x, 8 - o : 56 - o, :]
                if o % 2 == 0:
                    pair = pair + (fld[cur, 3 + x + o // 2, 8:56, :] + fld[cur, 3 + x - o // 2, 8:56, :])
                total = total + KIN[o] * pair
            total = ca * total
            if cb != 0.0:
                total = total + cb * center
            if cg != 0.0:
                total = total + cg * fld[prev, 3 + x, 8:56, :]
            fld[nxt, 3 + x, 8:56, :] = total
            return after

        lax.fori_loop(0, 32, local, odd(0))

        def outer(a, carry):
            xs = jnp.minimum(at_ref[1, a] // 2, 26)
            z0 = at_ref[0, a]
            win = (nxt, pl.ds(3 + xs, 6), pl.ds(8 + z0, 16), slice(None))
            fld[win] = fld[win] + scaled[pl.ds(a, 1), :][None] * tiles[pl.ds(6 * a, 6)]
            return carry

        lax.fori_loop(0, 64, outer, 0)

    def send(which, place):
        for i in range(32):
            zb, q = i // 4, i % 4
            for j in range(4):
                xp = 8 * q + 4 * core + j
                for kh in range(2):
                    z = 8 + 6 * zb + 3 * kh
                    to = ((2 * j + kh) * 32 + i) * 6 + place
                    out_ref[to : to + 3, :] = fld[which, 3 + xp, z : z + 3, :]

    step(0, 1, 2, 1.0 / HALF, -CENTER / HALF, 0.0)
    step(1, 2, 0, 2.0 / HALF, -2.0 * CENTER / HALF, -1.0)
    step(2, 0, 1, 2.0 / HALF, -2.0 * CENTER / HALF, -1.0)
    step(0, 1, 2, 2.0 / HALF, -2.0 * CENTER / HALF, -1.0)
    step(1, 2, 0, 1.0, 0.0, 0.0)
    send(1, 0)
    send(2, 3)


def y_taps():
    taps = np.zeros((128, 128), np.float32)
    for half in range(2):
        for y in range(NY):
            for o in range(1, 7):
                for to in (y - o, y + o):
                    if 0 <= to < NY:
                        taps[half * 64 + y, half * 64 + to] = KIN[o]
    return taps


def same_core():
    return [[2 * i + c for i in range(32)] for c in range(2)]


def same_core_all():
    return [[(2 * i + c) * 8 + y for y in range(8) for i in range(32)] for c in range(2)]


def x_groups():
    return [[16 * z + i for i in range(16)] for z in range(4)]


def zy_groups():
    return [[(16 * z + i) * 8 + y for z in range(4) for y in range(8)] for i in range(16)]


def pack(at, pos, proj, pot):
    return pl.pallas_call(
        pack_kernel,
        out_shape=jax.ShapeDtypeStruct((32, P1_ROWS, 128), F32),
        in_specs=[smem(), smem(), vmem(), vmem()],
        out_specs=vmem(),
        scratch_shapes=[pltpu.VMEM((64, 32, 128), F32)],
        compiler_params=params(),
        name="pack",
    )(at, pos, proj, pot)


def boxes(at, pos, got, orb):
    return pl.pallas_call(
        boxes_kernel,
        out_shape=jax.ShapeDtypeStruct((32, P2_ROWS, 128), F32),
        in_specs=[smem(), smem(), vmem(), vmem()],
        out_specs=vmem(),
        scratch_shapes=[pltpu.VMEM((2, 64, 128), F32)],
        compiler_params=params(),
        name="boxes",
    )(at, pos, got, orb)


def chebyshev(at, pos, strength, taps, own, oth, own_pot, oth_pot):
    return pl.pallas_call(
        filter_kernel,
        out_shape=jax.ShapeDtypeStruct((1536, 128), F32),
        in_specs=[smem(), smem()] + [vmem()] * 6,
        out_specs=vmem(),
        scratch_shapes=[
            pltpu.VMEM((3, 38, 64, 128), F32),
            pltpu.VMEM((32, 48, 128), F32),
            pltpu.VMEM((64 * 6, 16, 128), F32),
            pltpu.VMEM((64, 128), F32),
            pltpu.VMEM((64, 128), F32),
        ],
        compiler_params=params(),
        name="chebyshev",
    )(at, pos, strength, taps, own, oth, own_pot, oth_pot)


def swap_cores(values):
    return lax.ppermute(values, "dom", [(i, i ^ 1) for i in range(64)])


def sum_everywhere(values):
    mine = lax.all_to_all(values, "dom", 0, 0, tiled=True, axis_index_groups=x_groups())
    mine = jnp.sum(mine, axis=0)
    spread = jnp.broadcast_to(mine[None], (32,) + mine.shape)
    spread = lax.all_to_all(spread, ("dom", "band"), 0, 0, tiled=True, axis_index_groups=zy_groups())
    mine = jnp.sum(spread, axis=0)
    spread = jnp.broadcast_to(mine[None], (16,) + mine.shape)
    return lax.all_to_all(spread, "dom", 0, 0, tiled=True, axis_index_groups=x_groups())


def on_device(orbitals, potential, proj_shape, proj_strength, atom_z, atom_x, atom_y):
    me = lax.axis_index("dom")
    at = jnp.stack([atom_z, atom_x, atom_y])
    pos = jnp.stack([me // 8 * 6, me % 8 * 8, me // 2, me % 2]).astype(jnp.int32)
    strength = jnp.broadcast_to((proj_strength / PROJ_CELLS)[:, None], (64, 128))
    first = pack(at, pos, proj_shape.reshape(64, 24, 128), potential.reshape(24, 128))
    first = lax.all_to_all(first, "dom", 0, 0, tiled=True, axis_index_groups=same_core())
    first_oth = swap_cores(first)
    second = boxes(at, pos, first, orbitals.reshape(32, 24, 128))
    second = lax.all_to_all(second, "dom", 0, 0, tiled=True, axis_index_groups=same_core())
    second_oth = swap_cores(second)
    both = chebyshev(at, pos, strength, jnp.asarray(y_taps()), second, second_oth, first, first_oth)
    both = lax.all_to_all(both, ("dom", "band"), 0, 0, tiled=True, axis_index_groups=same_core_all())
    both = both.reshape(256, 6, 128)
    filtered = both[:, 0:3].reshape(256, 384)
    image = both[:, 3:6].reshape(256, 384)
    correlation = lax.dot_general(filtered, filtered, (((1,), (1,)), ((), ())), precision=HIGH)
    hamiltonian = lax.dot_general(filtered, image, (((1,), (1,)), ((), ())), precision=HIGH)
    total = sum_everywhere(jnp.stack([correlation, hamiltonian]).reshape(16, 64, 128))
    total = total.reshape(2, 256, 256) / NCELLS
    correlation, hamiltonian = total[0], total[1]
    lower = jnp.linalg.cholesky(correlation)
    inverse = lax.linalg.triangular_solve(lower, jnp.eye(256, dtype=F32), left_side=True, lower=True)
    projected = jnp.dot(jnp.dot(inverse, hamiltonian, precision=HIGH), inverse.T, precision=HIGH)
    projected = lax.dynamic_slice_in_dim(projected, 32 * lax.axis_index("band"), 32, 0)
    rotated = jnp.dot(inverse, filtered, precision=HIGH)
    rotated = lax.all_to_all(rotated.reshape(8, 96, 128), "band", 0, 0, tiled=True)
    rotated = rotated.reshape(4, 2, 32, 3, 128).transpose(2, 1, 3, 0, 4)
    return (rotated.reshape(32, 1, 6, 512), projected)


def solution(mesh):
    return jax.shard_map(
        on_device,
        mesh=mesh,
        in_specs=(
            P("band", "dom", None, None),
            P("dom", None, None),
            P(None, "dom", None, None),
            P(),
            P(),
            P(),
            P(),
        ),
        out_specs=(P("band", "dom", None, None), P("band", None)),
        check_vma=False,
    )
```

```python
import jax
import jax.numpy as jnp
import numpy as np
from jax import lax
from jax.experimental import pallas as pl
from jax.experimental.pallas import tpu as pltpu
from jax.sharding import PartitionSpec as P

NY = 64
NCELLS = 196608
PROJ_CELLS = 1000
COEFFS = [
    -5369.0 / 1800.0,
    12.0 / 7.0,
    -15.0 / 56.0,
    10.0 / 189.0,
    -1.0 / 112.0,
    2.0 / 1925.0,
    -1.0 / 16632.0,
]
CENTER = 9.5
HALF = 6.5
KIN = [-0.5 * c for c in COEFFS]
HIGH = lax.Precision.HIGHEST
F32 = jnp.float32


PIECE = 6
P1_ROWS = 40
BOX = 10
P2_ROWS = 48


def vmem():
    return pl.BlockSpec(memory_space=pltpu.VMEM)


def smem():
    return pl.BlockSpec(memory_space=pltpu.SMEM)


def params():
    return pltpu.CompilerParams(vmem_limit_bytes=56 * 1024 * 1024)


def pack_kernel(at_ref, pos_ref, proj_ref, pot_ref, out_ref, pad_ref):
    pad_ref[...] = jnp.zeros_like(pad_ref)
    pad_ref[:, 0:24, :] = proj_ref[...]
    lane = lax.broadcasted_iota(jnp.int32, (8, 128), 1)
    sub = lax.broadcasted_iota(jnp.int32, (8, 128), 0)
    z_cell = pos_ref[0] + sub
    x_first = pos_ref[1] + lane // 64
    slot = (lane % 64) // 16
    in_y = lane % 16 < 10

    def pair(i, carry):
        for m in range(2):
            a = 2 * i + m
            z0 = at_ref[0, a]
            x0 = at_ref[1, a]
            y0 = at_ref[2, a]
            in_z = (z_cell >= z0) & (z_cell < z0 + 10)
            packed = jnp.zeros((8, 128), F32)
            for j in range(4):
                x_cell = x_first + 2 * j
                inside = in_z & (x_cell >= x0) & (x_cell < x0 + 10)
                rows = pad_ref[a, pl.ds(j, 8, stride=4), :]
                rows = jnp.where(inside, rows, 0.0)
                rows = pltpu.roll(rows, (128 + 16 * j - y0) % 128, 1)
                packed = packed + jnp.where(in_y & (slot == j), rows, 0.0)
            out_ref[i, pl.ds(PIECE * m, PIECE), :] = packed[0:PIECE]
        out_ref[i, pl.ds(12, 24), :] = pot_ref[...]
        return carry

    lax.fori_loop(0, 32, pair, 0, unroll=4)


def boxes_kernel(at_ref, pos_ref, got_ref, orb_ref, out_ref, col_ref):
    col_ref[...] = jnp.zeros_like(col_ref)
    sub = lax.broadcasted_iota(jnp.int32, (16, 128), 0)
    for m in range(2):
        for zb in range(8):
            part = got_ref[4 * zb, PIECE * m : PIECE * (m + 1), :]
            for q in range(1, 4):
                part = part + got_ref[4 * zb + q, PIECE * m : PIECE * (m + 1), :]
            col_ref[m, 6 * zb : 6 * zb + 6, :] = part
    boxes = []
    for m in range(2):
        z0 = at_ref[0, 2 * pos_ref[2] + m]
        boxes.append(col_ref[m, pl.ds(z0, 16), :][0:BOX])

    def send(n, carry):
        out_ref[n, 0:BOX, :] = boxes[0]
        out_ref[n, BOX : 2 * BOX, :] = boxes[1]
        out_ref[n, 20:44, :] = orb_ref[n]
        out_ref[n, 44:48, :] = jnp.zeros((4, 128), F32)
        return carry

    lax.fori_loop(0, 32, send, 0)


def filter_kernel(
    at_ref, pos_ref, strength_ref, tapy_ref, tapz_ref, own_ref, oth_ref, ownp_ref, othp_ref, out_ref,
    fld, pot, tiles, parts, scaled,
):
    core = pos_ref[3]
    fld[...] = jnp.zeros_like(fld)
    tiles[...] = jnp.zeros_like(tiles)
    for src, src_pot, c in ((own_ref, ownp_ref, core), (oth_ref, othp_ref, 1 - core)):
        for i in range(32):
            zb, q = i // 4, i % 4
            for j in range(4):
                xp = 8 * q + 4 * c + j
                fld[0, 3 + xp, 8 + 6 * zb : 14 + 6 * zb, :] = src.at[i][pl.ds(20 + j, 6, stride=4), :]
                pot[xp, 6 * zb : 6 * zb + 6, :] = src_pot.at[i][pl.ds(12 + j, 6, stride=4), :]

    lane = lax.broadcasted_iota(jnp.int32, (BOX, 128), 1)
    slot = (lane % 64) // 16

    def expand(a, carry):
        xs = jnp.minimum(at_ref[1, a] // 2, 26)
        y0 = at_ref[2, a]
        start = BOX * (a % 2)
        own = own_ref[a // 2, pl.ds(start, BOX), :]
        oth = oth_ref[a // 2, pl.ds(start, BOX), :]
        for w in range(6):
            xp = xs + w
            j = xp % 4
            box = jnp.where((xp // 4) % 2 == core, own, oth)
            box = jnp.where(slot == j, box, 0.0)
            tiles[6 * a + w, 0:BOX, :] = pltpu.roll(box, (128 + y0 - 16 * j) % 128, 1)
        return carry

    lax.fori_loop(0, 64, expand, 0, unroll=8)

    ones = jnp.ones((128, 128), F32)
    low_half = lax.broadcasted_iota(jnp.int32, (8, 128), 1) < 64
    high_y = tapy_ref[:, 0:128]

    def step(cur, nxt, prev, ca, cb, cg):
        def inner(a, carry):
            xs = jnp.minimum(at_ref[1, a] // 2, 26)
            z0 = at_ref[0, a]
            win = fld[cur, pl.ds(3 + xs, 6), pl.ds(8 + z0, 16), :]
            prod = jnp.sum(win * tiles[pl.ds(6 * a, 6)], axis=0)
            parts[pl.ds(a, 1), :] = jnp.sum(prod, axis=0, keepdims=True)
            return carry

        lax.fori_loop(0, 64, inner, 0, unroll=8)
        sums = jnp.dot(parts[...], ones, precision=HIGH, preferred_element_type=F32)
        scaled[...] = sums * (ca * strength_ref[...])

        def along_yz(t, carry):
            rows = fld[cur, pl.ds(3 + 4 * t, 4), 8:56, :]
            high = rows.astype(jnp.bfloat16)
            rest = (rows - high.astype(F32)).astype(jnp.bfloat16)
            flat, flat_rest = high.reshape(192, 128), rest.reshape(192, 128)
            got = jnp.dot(flat, tapy_ref[...], preferred_element_type=F32)
            got = got[:, 0:128] + got[:, 128:256]
            got = got + jnp.dot(flat_rest, high_y, preferred_element_type=F32)
            wide = jnp.concatenate([high[n] for n in range(4)], axis=1)
            wide_rest = jnp.concatenate([rest[n] for n in range(4)], axis=1)
            by_z = jnp.dot(tapz_ref[...], wide, preferred_element_type=F32)
            by_z = by_z[0:48] + by_z[48:96]
            by_z = by_z + jnp.dot(tapz_ref[0:48, :], wide_rest, preferred_element_type=F32)
            for n in range(4):
                fld[nxt, 3 + 4 * t + n, 8:56, :] = got[48 * n : 48 * n + 48] + by_z[:, 128 * n : 128 * n + 128]
            return carry

        lax.fori_loop(0, 8, along_yz, 0)

        def along_x(zt, carry):
            rows = pl.ds(pl.multiple_of(8 + 8 * zt, 8), 8)
            own_rows = pl.ds(pl.multiple_of(8 * zt, 8), 8)
            zero = jnp.zeros((8, 128), F32)
            line = {x: zero for x in (-3, -2, -1, 32, 33, 34, 35)}
            for x in range(3):
                line[x] = fld[cur, 3 + x, rows, :]

            def odd(x):
                total = KIN[1] * (line[x] + line[x - 1]) + KIN[3] * (line[x + 1] + line[x - 2])
                total = total + KIN[5] * (line[x + 2] + line[x - 3])
                return pltpu.roll(total, 64, 1)

            here = odd(0)
            for x in range(32):
                if x + 3 < 32:
                    line[x + 3] = fld[cur, 6 + x, rows, :]
                after = odd(x + 1)
                total = fld[nxt, 3 + x, rows, :] + jnp.where(low_half, here, after)
                total = total + (3.0 * KIN[0] + pot[x, own_rows, :]) * line[x]
                for o in (1, 2, 3):
                    total = total + KIN[2 * o] * (line[x + o] + line[x - o])
                total = ca * total
                if cb != 0.0:
                    total = total + cb * line[x]
                if cg != 0.0:
                    total = total + cg * fld[prev, 3 + x, rows, :]
                fld[nxt, 3 + x, rows, :] = total
                here = after
            return carry

        lax.fori_loop(0, 6, along_x, 0)

        def outer(a, carry):
            xs = jnp.minimum(at_ref[1, a] // 2, 26)
            z0 = at_ref[0, a]
            win = (nxt, pl.ds(3 + xs, 6), pl.ds(8 + z0, 16), slice(None))
            fld[win] = fld[win] + scaled[pl.ds(a, 1), :][None] * tiles[pl.ds(6 * a, 6)]
            return carry

        lax.fori_loop(0, 64, outer, 0, unroll=4)

    def send(which, place):
        for i in range(32):
            zb, q = i // 4, i % 4
            for j in range(4):
                xp = 8 * q + 4 * core + j
                for kh in range(2):
                    z = 8 + 6 * zb + 3 * kh
                    to = ((2 * j + kh) * 32 + i) * 6 + place
                    out_ref[to : to + 3, :] = fld[which, 3 + xp, z : z + 3, :]

    step(0, 1, 2, 1.0 / HALF, -CENTER / HALF, 0.0)
    step(1, 2, 0, 2.0 / HALF, -2.0 * CENTER / HALF, -1.0)
    step(2, 0, 1, 2.0 / HALF, -2.0 * CENTER / HALF, -1.0)
    step(0, 1, 2, 2.0 / HALF, -2.0 * CENTER / HALF, -1.0)
    step(1, 2, 0, 1.0, 0.0, 0.0)
    send(1, 0)
    send(2, 3)


def band_matrix(n, blocks):
    taps = np.zeros((n * blocks, n * blocks), np.float32)
    for b in range(blocks):
        for k in range(n):
            for o in range(1, 7):
                for to in (k - o, k + o):
                    if 0 <= to < n:
                        taps[b * n + k, b * n + to] = KIN[o]
    return taps


def two_parts(taps, axis):
    high = jnp.asarray(taps).astype(jnp.bfloat16)
    rest = (jnp.asarray(taps) - high.astype(F32)).astype(jnp.bfloat16)
    return jnp.concatenate([high, rest], axis=axis)


def same_core():
    return [[2 * i + c for i in range(32)] for c in range(2)]


def same_core_all():
    return [[(2 * i + c) * 8 + y for y in range(8) for i in range(32)] for c in range(2)]


def x_groups():
    return [[16 * z + i for i in range(16)] for z in range(4)]


def zy_groups():
    return [[(16 * z + i) * 8 + y for z in range(4) for y in range(8)] for i in range(16)]


def pack(at, pos, proj, pot):
    return pl.pallas_call(
        pack_kernel,
        out_shape=jax.ShapeDtypeStruct((32, P1_ROWS, 128), F32),
        in_specs=[smem(), smem(), vmem(), vmem()],
        out_specs=vmem(),
        scratch_shapes=[pltpu.VMEM((64, 32, 128), F32)],
        compiler_params=params(),
        name="pack",
    )(at, pos, proj, pot)


def boxes(at, pos, got, orb):
    return pl.pallas_call(
        boxes_kernel,
        out_shape=jax.ShapeDtypeStruct((32, P2_ROWS, 128), F32),
        in_specs=[smem(), smem(), vmem(), vmem()],
        out_specs=vmem(),
        scratch_shapes=[pltpu.VMEM((2, 64, 128), F32)],
        compiler_params=params(),
        name="boxes",
    )(at, pos, got, orb)


def chebyshev(at, pos, strength, own, oth, own_pot, oth_pot):
    tapy = two_parts(band_matrix(NY, 2), 1)
    tapz = two_parts(band_matrix(48, 1), 0)
    return pl.pallas_call(
        filter_kernel,
        out_shape=jax.ShapeDtypeStruct((1536, 128), F32),
        in_specs=[smem(), smem()] + [vmem()] * 7,
        out_specs=vmem(),
        scratch_shapes=[
            pltpu.VMEM((3, 38, 64, 128), F32),
            pltpu.VMEM((32, 48, 128), F32),
            pltpu.VMEM((64 * 6, 16, 128), F32),
            pltpu.VMEM((64, 128), F32),
            pltpu.VMEM((64, 128), F32),
        ],
        compiler_params=params(),
        name="chebyshev",
    )(at, pos, strength, tapy, tapz, own, oth, own_pot, oth_pot)


def dot(a, b):
    return jnp.dot(a, b, precision=HIGH, preferred_element_type=F32)


def dot_t(a, b):
    return lax.dot_general(a, b, (((1,), (1,)), ((), ())), precision=HIGH, preferred_element_type=F32)


def gram_kernel(both_ref, out_ref):
    f = [both_ref[pl.ds(r, 256, stride=6), :] for r in range(3)]
    g = [both_ref[pl.ds(3 + r, 256, stride=6), :] for r in range(3)]
    f = jnp.concatenate(f, axis=1)
    g = jnp.concatenate(g, axis=1)
    corr = dot_t(f, f)
    ham = dot_t(f, g)
    row = lax.broadcasted_iota(jnp.int32, (256, 256), 0)
    col = lax.broadcasted_iota(jnp.int32, (256, 256), 1)
    packed = jnp.where(row >= col, corr, ham)
    diag = jnp.sum(jnp.where(row == col, ham, 0.0), axis=0, keepdims=True)
    out_ref[...] = jnp.zeros_like(out_ref)
    for q in range(16):
        out_ref[q, 0:16, :] = packed[16 * q : 16 * q + 16, 0:128]
        out_ref[q, 16:32, :] = packed[16 * q : 16 * q + 16, 128:256]
    out_ref[0, 32:33, :] = diag[:, 0:128]
    out_ref[0, 33:34, :] = diag[:, 128:256]


def ortho_kernel(pos_ref, total_ref, both_ref, rot_ref, proj_ref, corr, ham, inv, work):
    row = lax.broadcasted_iota(jnp.int32, (256, 256), 0)
    col = lax.broadcasted_iota(jnp.int32, (256, 256), 1)
    below = row > col
    same = row == col
    scale = 1.0 / NCELLS
    for q in range(16):
        work[16 * q : 16 * q + 16, 0:128] = total_ref[q, 0:16, :]
        work[16 * q : 16 * q + 16, 128:256] = total_ref[q, 16:32, :]
    packed = work[...] * scale
    turned = packed.T
    diag = jnp.concatenate([total_ref[0, 32:33, :], total_ref[0, 33:34, :]], axis=1) * scale
    corr[...] = jnp.where(row >= col, packed, turned)
    ham[...] = jnp.where(same, diag, jnp.where(below, turned, packed))

    def half_lower(e):
        return jnp.where(below, e, jnp.where(same, 0.5 * e, 0.0))

    own = jnp.where(same, corr[...], 0.0)
    by_col = lax.rsqrt(jnp.sum(own, axis=0, keepdims=True))
    by_row = lax.rsqrt(jnp.sum(own, axis=1, keepdims=True))
    first = half_lower(by_row * corr[...] * by_col - jnp.where(same, 1.0, 0.0))
    inv[...] = jnp.where(same, by_col, 0.0) - first * by_col

    def rough(a, b, turn=False):
        dims = (((1,), (1 if turn else 0,)), ((), ()))
        return lax.dot_general(
            a.astype(jnp.bfloat16), b.astype(jnp.bfloat16), dims, preferred_element_type=F32
        )

    for _ in range(2):
        x = inv[...]
        e = rough(rough(x, corr[...]), x, True) - jnp.where(same, 1.0, 0.0)
        inv[...] = x - rough(half_lower(e), x)

    def refine(state):
        count, _ = state
        x = inv[...]
        e = dot_t(dot(x, corr[...]), x) - jnp.where(same, 1.0, 0.0)
        inv[...] = x - dot(half_lower(e), x)
        return count + 1, jnp.sum(e * e)

    def going(state):
        count, size = state
        return (count < 8) & jnp.logical_not(size < 1e-8)

    _, size = lax.while_loop(going, refine, (jnp.int32(0), jnp.float32(1.0)))
    least = jnp.min(jnp.where(same, inv[...], 1.0))

    @pl.when(jnp.logical_not((size < 1e-8) & (least > 0.0)))
    def _():
        work[...] = corr[...]
        inv[...] = jnp.where(same, 1.0, 0.0)

        def column(j, carry):
            picked = jnp.sum(jnp.where(col == j, work[...], 0.0), axis=1, keepdims=True)
            at_j = lax.broadcasted_iota(jnp.int32, (256, 1), 0)
            pivot = jnp.sum(jnp.where(at_j == j, picked, 0.0), axis=0, keepdims=True)
            factor = 1.0 / jnp.sqrt(pivot)
            inv[pl.ds(j, 1), :] = inv[pl.ds(j, 1), :] * factor
            down = jnp.where(at_j > j, picked, 0.0) * factor
            work[...] = work[...] - down * (work[pl.ds(j, 1), :] * factor)
            inv[...] = inv[...] - down * inv[pl.ds(j, 1), :]
            return carry

        lax.fori_loop(0, 256, column, 0)

    x = inv[...]
    mine = inv[pl.ds(pl.multiple_of(32 * pos_ref[4], 32), 32), :]
    proj_ref[...] = dot_t(dot(mine, ham[...]), x)
    for r in range(3):
        part = dot(x, both_ref[pl.ds(r, 256, stride=6), :])
        rot_ref[pl.ds(r, 256, stride=3), :] = part


def gram(both):
    return pl.pallas_call(
        gram_kernel,
        out_shape=jax.ShapeDtypeStruct((16, 40, 128), F32),
        in_specs=[vmem()],
        out_specs=vmem(),
        compiler_params=params(),
        name="gram",
    )(both)


def ortho(pos, total, both):
    return pl.pallas_call(
        ortho_kernel,
        out_shape=[jax.ShapeDtypeStruct((768, 128), F32), jax.ShapeDtypeStruct((32, 256), F32)],
        in_specs=[smem(), vmem(), vmem()],
        out_specs=[vmem(), vmem()],
        scratch_shapes=[pltpu.VMEM((256, 256), F32)] * 4,
        compiler_params=params(),
        name="ortho",
    )(pos, total, both)


def swap_cores(values):
    return lax.ppermute(values, "dom", [(i, i ^ 1) for i in range(64)])


def sum_everywhere(values):
    mine = lax.all_to_all(values, "dom", 0, 0, tiled=True, axis_index_groups=x_groups())
    mine = jnp.sum(mine, axis=0)
    spread = jnp.broadcast_to(mine[None], (32,) + mine.shape)
    spread = lax.all_to_all(spread, ("dom", "band"), 0, 0, tiled=True, axis_index_groups=zy_groups())
    mine = jnp.sum(spread, axis=0)
    spread = jnp.broadcast_to(mine[None], (16,) + mine.shape)
    return lax.all_to_all(spread, "dom", 0, 0, tiled=True, axis_index_groups=x_groups())


def on_device(orbitals, potential, proj_shape, proj_strength, atom_z, atom_x, atom_y):
    me = lax.axis_index("dom")
    at = jnp.stack([atom_z, atom_x, atom_y])
    pos = jnp.stack([me // 8 * 6, me % 8 * 8, me // 2, me % 2, lax.axis_index("band")]).astype(jnp.int32)
    strength = jnp.broadcast_to((proj_strength / PROJ_CELLS)[:, None], (64, 128))
    first = pack(at, pos, proj_shape.reshape(64, 24, 128), potential.reshape(24, 128))
    first = lax.all_to_all(first, "dom", 0, 0, tiled=True, axis_index_groups=same_core())
    first_oth = swap_cores(first)
    second = boxes(at, pos, first, orbitals.reshape(32, 24, 128))
    second = lax.all_to_all(second, "dom", 0, 0, tiled=True, axis_index_groups=same_core())
    second_oth = swap_cores(second)
    both = chebyshev(at, pos, strength, second, second_oth, first, first_oth)
    both = lax.all_to_all(both, ("dom", "band"), 0, 0, tiled=True, axis_index_groups=same_core_all())
    total = sum_everywhere(gram(both))
    rotated, projected = ortho(pos, total, both)
    rotated = lax.all_to_all(rotated.reshape(8, 96, 128), "band", 0, 0, tiled=True)
    rotated = rotated.reshape(4, 2, 32, 3, 128).transpose(2, 1, 3, 0, 4)
    return (rotated.reshape(32, 1, 6, 512), projected)


def solution(mesh):
    return jax.shard_map(
        on_device,
        mesh=mesh,
        in_specs=(
            P("band", "dom", None, None),
            P("dom", None, None),
            P(None, "dom", None, None),
            P(),
            P(),
            P(),
            P(),
        ),
        out_specs=(P("band", "dom", None, None), P("band", None)),
        check_vma=False,
    )
```

```python
import jax
import jax.numpy as jnp
import numpy as np
from jax import lax
from jax.experimental import pallas as pl
from jax.experimental.pallas import tpu as pltpu
from jax.sharding import PartitionSpec as P

NY = 64
NCELLS = 196608
PROJ_CELLS = 1000
COEFFS = [
    -5369.0 / 1800.0,
    12.0 / 7.0,
    -15.0 / 56.0,
    10.0 / 189.0,
    -1.0 / 112.0,
    2.0 / 1925.0,
    -1.0 / 16632.0,
]
CENTER = 9.5
HALF = 6.5
KIN = [-0.5 * c for c in COEFFS]
HIGH = lax.Precision.HIGHEST
F32 = jnp.float32


P1_ROWS = 32
P2_ROWS = 40


def vmem():
    return pl.BlockSpec(memory_space=pltpu.VMEM)


def smem():
    return pl.BlockSpec(memory_space=pltpu.SMEM)


def params():
    return pltpu.CompilerParams(vmem_limit_bytes=56 * 1024 * 1024)


def pack_kernel(at_ref, pos_ref, proj_ref, pot_ref, out_ref, pad_ref):
    pad_ref[:, 24:48, :] = jnp.zeros((64, 24, 128), F32)
    pad_ref[:, 0:24, :] = proj_ref[...]
    lane = lax.broadcasted_iota(jnp.int32, (8, 128), 1)
    sub = lax.broadcasted_iota(jnp.int32, (8, 128), 0)
    slot_lane = lane % 64
    z_cells, x_cells, slots = [], [], []
    for s in range(6):
        row = s + 6 * sub
        z_cells.append(pos_ref[0] + row // 4)
        x_cells.append(pos_ref[1] + 2 * (row % 4) + lane // 64)
        slots.append((slot_lane >= 10 * s) & (slot_lane < 10 * s + 10))

    def pair(i, carry):
        for m in range(2):
            a = 2 * i + m
            z0 = at_ref[0, a]
            x0 = at_ref[1, a]
            y0 = at_ref[2, a]
            packed = jnp.zeros((8, 128), F32)
            for s in range(6):
                z, x = z_cells[s], x_cells[s]
                inside = (z >= z0) & (z < z0 + 10) & (x >= x0) & (x < x0 + 10)
                rows = pad_ref[a, pl.ds(s, 8, stride=6), :]
                rows = jnp.where(inside, rows, 0.0)
                rows = pltpu.roll(rows, (128 + 10 * s - y0) & 127, 1)
                packed = jnp.where(slots[s], rows, packed)
            out_ref[i, pl.ds(4 * m, 4), :] = packed[0:4]
        out_ref[i, pl.ds(8, 24), :] = pot_ref[...]
        return carry

    lax.fori_loop(0, 32, pair, 0, unroll=4)


def first_row(z0):
    return (4 * z0 * 171) >> 10


def boxes_kernel(at_ref, pos_ref, got_ref, orb_ref, out_ref, col_ref):
    col_ref[...] = jnp.zeros_like(col_ref)
    for zb in range(8):
        part = got_ref[4 * zb, 0:8, :]
        for q in range(1, 4):
            part = part + got_ref[4 * zb + q, 0:8, :]
        col_ref[0, 4 * zb : 4 * zb + 4, :] = part[0:4]
        col_ref[1, 4 * zb : 4 * zb + 4, :] = part[4:8]
    boxes = []
    for m in range(2):
        z0 = at_ref[0, 2 * pos_ref[2] + m]
        boxes.append(col_ref[m, pl.ds(first_row(z0), 8), :])

    def send(n, carry):
        out_ref[n, 0:8, :] = boxes[0]
        out_ref[n, 8:16, :] = boxes[1]
        out_ref[n, 16:40, :] = orb_ref[n]
        return carry

    lax.fori_loop(0, 32, send, 0, unroll=4)


def filter_kernel(
    at_ref, pos_ref, strength_ref, tapy_ref, tapz_ref, own_ref, oth_ref, ownp_ref, othp_ref, out_ref,
    fld, pot, half, tiles, parts, scaled,
):
    core = pos_ref[3]
    fld[...] = jnp.zeros_like(fld)
    tiles[...] = jnp.zeros_like(tiles)
    for src, src_pot, c in ((own_ref, ownp_ref, core), (oth_ref, othp_ref, 1 - core)):
        for i in range(32):
            zb, q = i // 4, i % 4
            for j in range(4):
                xp = 8 * q + 4 * c + j
                fld[0, 3 + xp, 8 + 6 * zb : 14 + 6 * zb, :] = src.at[i][pl.ds(16 + j, 6, stride=4), :]
                pot[xp, 6 * zb : 6 * zb + 6, :] = src_pot.at[i][pl.ds(8 + j, 6, stride=4), :]

    half[pl.ds(core, 1)] = own_ref[:, 0:16, :].reshape(1, 64, 8, 128)
    half[pl.ds(1 - core, 1)] = oth_ref[:, 0:16, :].reshape(1, 64, 8, 128)
    slot_lane = lax.broadcasted_iota(jnp.int32, (4, 128), 1) & 63

    def expand(a, carry):
        xs = jnp.minimum(at_ref[1, a] >> 1, 26)
        y0 = at_ref[2, a]
        z0 = at_ref[0, a]
        begin = 4 * z0 - 6 * first_row(z0)
        for w in range(6):
            xp = xs + w
            for v in range(3):
                n = 4 if v == 0 else 3
                place = begin + (xp & 3) + 4 * v
                row = (place * 11) >> 6
                left = 10 * (place - 6 * row)
                box = half[(xp >> 2) & 1, a, pl.ds(row, n, stride=2), :]
                in_slot = (slot_lane[0:n] >= left) & (slot_lane[0:n] < left + 10)
                box = jnp.where(in_slot, box, 0.0)
                tiles[6 * a + w, pl.ds(v, n, stride=3), :] = pltpu.roll(box, (128 + y0 - left) & 127, 1)
        return carry

    lax.fori_loop(0, 64, expand, 0, unroll=4)

    ones = jnp.ones((128, 128), F32)
    low_half = lax.broadcasted_iota(jnp.int32, (8, 128), 1) < 64
    high_y = tapy_ref[:, 0:128]

    def step(cur, nxt, prev, ca, cb, cg):
        def inner(a, carry):
            xs = jnp.minimum(at_ref[1, a] >> 1, 26)
            z0 = at_ref[0, a]
            win = fld[cur, pl.ds(3 + xs, 6), pl.ds(8 + z0, 16), :]
            prod = jnp.sum(win * tiles[pl.ds(6 * a, 6)], axis=0)
            parts[pl.ds(a, 1), :] = jnp.sum(prod, axis=0, keepdims=True)
            return carry

        lax.fori_loop(0, 64, inner, 0, unroll=8)
        sums = jnp.dot(parts[...], ones, precision=HIGH, preferred_element_type=F32)
        scaled[...] = sums * (ca * strength_ref[...])

        def along_yz(t, carry):
            rows = fld[cur, pl.ds(3 + 4 * t, 4), 8:56, :]
            high = rows.astype(jnp.bfloat16)
            rest = (rows - high.astype(F32)).astype(jnp.bfloat16)
            flat, flat_rest = high.reshape(192, 128), rest.reshape(192, 128)
            got = jnp.dot(flat, tapy_ref[...], preferred_element_type=F32)
            got = got[:, 0:128] + got[:, 128:256]
            got = got + jnp.dot(flat_rest, high_y, preferred_element_type=F32)
            wide = jnp.concatenate([high[n] for n in range(4)], axis=1)
            wide_rest = jnp.concatenate([rest[n] for n in range(4)], axis=1)
            by_z = jnp.dot(tapz_ref[...], wide, preferred_element_type=F32)
            by_z = by_z[0:48] + by_z[48:96]
            by_z = by_z + jnp.dot(tapz_ref[0:48, :], wide_rest, preferred_element_type=F32)
            for n in range(4):
                fld[nxt, 3 + 4 * t + n, 8:56, :] = got[48 * n : 48 * n + 48] + by_z[:, 128 * n : 128 * n + 128]
            return carry

        lax.fori_loop(0, 8, along_yz, 0, unroll=8)

        def along_x(zt, carry):
            rows = pl.ds(pl.multiple_of(8 + 8 * zt, 8), 8)
            own_rows = pl.ds(pl.multiple_of(8 * zt, 8), 8)
            zero = jnp.zeros((8, 128), F32)
            line = {x: zero for x in (-3, -2, -1, 32, 33, 34, 35)}
            for x in range(3):
                line[x] = fld[cur, 3 + x, rows, :]

            def odd(x):
                total = KIN[1] * (line[x] + line[x - 1]) + KIN[3] * (line[x + 1] + line[x - 2])
                total = total + KIN[5] * (line[x + 2] + line[x - 3])
                return pltpu.roll(total, 64, 1)

            here = odd(0)
            for x in range(32):
                if x + 3 < 32:
                    line[x + 3] = fld[cur, 6 + x, rows, :]
                after = odd(x + 1)
                total = fld[nxt, 3 + x, rows, :] + jnp.where(low_half, here, after)
                total = total + (3.0 * KIN[0] + pot[x, own_rows, :]) * line[x]
                for o in (1, 2, 3):
                    total = total + KIN[2 * o] * (line[x + o] + line[x - o])
                total = ca * total
                if cb != 0.0:
                    total = total + cb * line[x]
                if cg != 0.0:
                    total = total + cg * fld[prev, 3 + x, rows, :]
                fld[nxt, 3 + x, rows, :] = total
                here = after
            return carry

        lax.fori_loop(0, 6, along_x, 0)

        def outer(a, carry):
            xs = jnp.minimum(at_ref[1, a] >> 1, 26)
            z0 = at_ref[0, a]
            win = (nxt, pl.ds(3 + xs, 6), pl.ds(8 + z0, 16), slice(None))
            fld[win] = fld[win] + scaled[pl.ds(a, 1), :][None] * tiles[pl.ds(6 * a, 6)]
            return carry

        lax.fori_loop(0, 64, outer, 0, unroll=4)

    def send(which, place):
        for i in range(32):
            zb, q = i // 4, i % 4
            for j in range(4):
                xp = 8 * q + 4 * core + j
                for kh in range(2):
                    z = 8 + 6 * zb + 3 * kh
                    to = ((2 * j + kh) * 32 + i) * 6 + place
                    out_ref[to : to + 3, :] = fld[which, 3 + xp, z : z + 3, :]

    step(0, 1, 2, 1.0 / HALF, -CENTER / HALF, 0.0)
    step(1, 2, 0, 2.0 / HALF, -2.0 * CENTER / HALF, -1.0)
    step(2, 0, 1, 2.0 / HALF, -2.0 * CENTER / HALF, -1.0)
    step(0, 1, 2, 2.0 / HALF, -2.0 * CENTER / HALF, -1.0)
    step(1, 2, 0, 1.0, 0.0, 0.0)
    send(1, 0)
    send(2, 3)


def band_matrix(n, blocks):
    taps = np.zeros((n * blocks, n * blocks), np.float32)
    for b in range(blocks):
        for k in range(n):
            for o in range(1, 7):
                for to in (k - o, k + o):
                    if 0 <= to < n:
                        taps[b * n + k, b * n + to] = KIN[o]
    return taps


def two_parts(taps, axis):
    high = jnp.asarray(taps).astype(jnp.bfloat16)
    rest = (jnp.asarray(taps) - high.astype(F32)).astype(jnp.bfloat16)
    return jnp.concatenate([high, rest], axis=axis)


def same_core():
    return [[2 * i + c for i in range(32)] for c in range(2)]


def same_core_all():
    return [[(2 * i + c) * 8 + y for y in range(8) for i in range(32)] for c in range(2)]


def x_groups():
    return [[16 * z + i for i in range(16)] for z in range(4)]


def zy_groups():
    return [[(16 * z + i) * 8 + y for z in range(4) for y in range(8)] for i in range(16)]


def pack(at, pos, proj, pot):
    return pl.pallas_call(
        pack_kernel,
        out_shape=jax.ShapeDtypeStruct((32, P1_ROWS, 128), F32),
        in_specs=[smem(), smem(), vmem(), vmem()],
        out_specs=vmem(),
        scratch_shapes=[pltpu.VMEM((64, 48, 128), F32)],
        compiler_params=params(),
        name="pack",
    )(at, pos, proj, pot)


def boxes(at, pos, got, orb):
    return pl.pallas_call(
        boxes_kernel,
        out_shape=jax.ShapeDtypeStruct((32, P2_ROWS, 128), F32),
        in_specs=[smem(), smem(), vmem(), vmem()],
        out_specs=vmem(),
        scratch_shapes=[pltpu.VMEM((2, 40, 128), F32)],
        compiler_params=params(),
        name="boxes",
    )(at, pos, got, orb)


def chebyshev(at, pos, strength, own, oth, own_pot, oth_pot):
    tapy = two_parts(band_matrix(NY, 2), 1)
    tapz = two_parts(band_matrix(48, 1), 0)
    return pl.pallas_call(
        filter_kernel,
        out_shape=jax.ShapeDtypeStruct((1536, 128), F32),
        in_specs=[smem(), smem()] + [vmem()] * 7,
        out_specs=vmem(),
        scratch_shapes=[
            pltpu.VMEM((3, 38, 64, 128), F32),
            pltpu.VMEM((32, 48, 128), F32),
            pltpu.VMEM((2, 64, 8, 128), F32),
            pltpu.VMEM((64 * 6, 16, 128), F32),
            pltpu.VMEM((64, 128), F32),
            pltpu.VMEM((64, 128), F32),
        ],
        compiler_params=params(),
        name="chebyshev",
    )(at, pos, strength, tapy, tapz, own, oth, own_pot, oth_pot)


def dot(a, b):
    return jnp.dot(a, b, precision=HIGH, preferred_element_type=F32)


def dot_t(a, b):
    return lax.dot_general(a, b, (((1,), (1,)), ((), ())), precision=HIGH, preferred_element_type=F32)


def gram_kernel(both_ref, out_ref):
    f = [both_ref[pl.ds(r, 256, stride=6), :] for r in range(3)]
    g = [both_ref[pl.ds(3 + r, 256, stride=6), :] for r in range(3)]
    f = jnp.concatenate(f, axis=1)
    g = jnp.concatenate(g, axis=1)
    corr = dot_t(f, f)
    ham = dot_t(f, g)
    row = lax.broadcasted_iota(jnp.int32, (256, 256), 0)
    col = lax.broadcasted_iota(jnp.int32, (256, 256), 1)
    packed = jnp.where(row >= col, corr, ham)
    diag = jnp.sum(jnp.where(row == col, ham, 0.0), axis=0, keepdims=True)
    out_ref[...] = jnp.zeros_like(out_ref)
    for q in range(16):
        out_ref[q, 0:16, :] = packed[16 * q : 16 * q + 16, 0:128]
        out_ref[q, 16:32, :] = packed[16 * q : 16 * q + 16, 128:256]
    out_ref[0, 32:33, :] = diag[:, 0:128]
    out_ref[0, 33:34, :] = diag[:, 128:256]


def ortho_kernel(pos_ref, total_ref, both_ref, rot_ref, proj_ref, corr, ham, inv, work):
    row = lax.broadcasted_iota(jnp.int32, (256, 256), 0)
    col = lax.broadcasted_iota(jnp.int32, (256, 256), 1)
    below = row > col
    same = row == col
    scale = 1.0 / NCELLS
    for q in range(16):
        work[16 * q : 16 * q + 16, 0:128] = total_ref[q, 0:16, :]
        work[16 * q : 16 * q + 16, 128:256] = total_ref[q, 16:32, :]
    packed = work[...] * scale
    turned = packed.T
    diag = jnp.concatenate([total_ref[0, 32:33, :], total_ref[0, 33:34, :]], axis=1) * scale
    corr[...] = jnp.where(row >= col, packed, turned)
    ham[...] = jnp.where(same, diag, jnp.where(below, turned, packed))

    def half_lower(e):
        return jnp.where(below, e, jnp.where(same, 0.5 * e, 0.0))

    own = jnp.where(same, corr[...], 0.0)
    by_col = lax.rsqrt(jnp.sum(own, axis=0, keepdims=True))
    by_row = lax.rsqrt(jnp.sum(own, axis=1, keepdims=True))
    first = half_lower(by_row * corr[...] * by_col - jnp.where(same, 1.0, 0.0))
    inv[...] = jnp.where(same, by_col, 0.0) - first * by_col

    def rough(a, b, turn=False):
        dims = (((1,), (1 if turn else 0,)), ((), ()))
        return lax.dot_general(
            a.astype(jnp.bfloat16), b.astype(jnp.bfloat16), dims, preferred_element_type=F32
        )

    for _ in range(2):
        x = inv[...]
        e = rough(rough(x, corr[...]), x, True) - jnp.where(same, 1.0, 0.0)
        inv[...] = x - rough(half_lower(e), x)

    def refine(state):
        count, _ = state
        x = inv[...]
        e = dot_t(dot(x, corr[...]), x) - jnp.where(same, 1.0, 0.0)
        inv[...] = x - dot(half_lower(e), x)
        return count + 1, jnp.sum(e * e)

    def going(state):
        count, size = state
        return (count < 8) & jnp.logical_not(size < 1e-8)

    _, size = lax.while_loop(going, refine, (jnp.int32(0), jnp.float32(1.0)))
    least = jnp.min(jnp.where(same, inv[...], 1.0))

    @pl.when(jnp.logical_not((size < 1e-8) & (least > 0.0)))
    def _():
        work[...] = corr[...]
        inv[...] = jnp.where(same, 1.0, 0.0)

        def column(j, carry):
            picked = jnp.sum(jnp.where(col == j, work[...], 0.0), axis=1, keepdims=True)
            at_j = lax.broadcasted_iota(jnp.int32, (256, 1), 0)
            pivot = jnp.sum(jnp.where(at_j == j, picked, 0.0), axis=0, keepdims=True)
            factor = 1.0 / jnp.sqrt(pivot)
            inv[pl.ds(j, 1), :] = inv[pl.ds(j, 1), :] * factor
            down = jnp.where(at_j > j, picked, 0.0) * factor
            work[...] = work[...] - down * (work[pl.ds(j, 1), :] * factor)
            inv[...] = inv[...] - down * inv[pl.ds(j, 1), :]
            return carry

        lax.fori_loop(0, 256, column, 0)

    x = inv[...]
    mine = inv[pl.ds(pl.multiple_of(32 * pos_ref[4], 32), 32), :]
    proj_ref[...] = dot_t(dot(mine, ham[...]), x)
    for r in range(3):
        part = dot(x, both_ref[pl.ds(r, 256, stride=6), :])
        rot_ref[pl.ds(r, 256, stride=3), :] = part


def gram(both):
    return pl.pallas_call(
        gram_kernel,
        out_shape=jax.ShapeDtypeStruct((16, 40, 128), F32),
        in_specs=[vmem()],
        out_specs=vmem(),
        compiler_params=params(),
        name="gram",
    )(both)


def ortho(pos, total, both):
    return pl.pallas_call(
        ortho_kernel,
        out_shape=[jax.ShapeDtypeStruct((768, 128), F32), jax.ShapeDtypeStruct((32, 256), F32)],
        in_specs=[smem(), vmem(), vmem()],
        out_specs=[vmem(), vmem()],
        scratch_shapes=[pltpu.VMEM((256, 256), F32)] * 4,
        compiler_params=params(),
        name="ortho",
    )(pos, total, both)


def swap_cores(values):
    return lax.ppermute(values, "dom", [(i, i ^ 1) for i in range(64)])


def sum_everywhere(values):
    mine = lax.all_to_all(values, "dom", 0, 0, tiled=True, axis_index_groups=x_groups())
    mine = jnp.sum(mine, axis=0)
    spread = jnp.broadcast_to(mine[None], (32,) + mine.shape)
    spread = lax.all_to_all(spread, ("dom", "band"), 0, 0, tiled=True, axis_index_groups=zy_groups())
    mine = jnp.sum(spread, axis=0)
    spread = jnp.broadcast_to(mine[None], (16,) + mine.shape)
    return lax.all_to_all(spread, "dom", 0, 0, tiled=True, axis_index_groups=x_groups())


def on_device(orbitals, potential, proj_shape, proj_strength, atom_z, atom_x, atom_y):
    me = lax.axis_index("dom")
    at = jnp.stack([atom_z, atom_x, atom_y])
    pos = jnp.stack([me // 8 * 6, me % 8 * 8, me // 2, me % 2, lax.axis_index("band")]).astype(jnp.int32)
    strength = jnp.broadcast_to((proj_strength / PROJ_CELLS)[:, None], (64, 128))
    first = pack(at, pos, proj_shape.reshape(64, 24, 128), potential.reshape(24, 128))
    first = lax.all_to_all(first, "dom", 0, 0, tiled=True, axis_index_groups=same_core())
    first_oth = swap_cores(first)
    second = boxes(at, pos, first, orbitals.reshape(32, 24, 128))
    second = lax.all_to_all(second, "dom", 0, 0, tiled=True, axis_index_groups=same_core())
    second_oth = swap_cores(second)
    both = chebyshev(at, pos, strength, second, second_oth, first, first_oth)
    both = both.reshape(256, 3, 2, 128)
    both = lax.all_to_all(both, ("dom", "band"), 0, 0, tiled=True, axis_index_groups=same_core_all())
    both = both.reshape(1536, 128)
    total = sum_everywhere(gram(both))
    rotated, projected = ortho(pos, total, both)
    rotated = lax.all_to_all(rotated.reshape(8, 96, 128), "band", 0, 0, tiled=True)
    rotated = rotated.reshape(4, 2, 32, 3, 128).transpose(2, 1, 3, 0, 4)
    return (rotated.reshape(32, 1, 6, 512), projected)


def solution(mesh):
    return jax.shard_map(
        on_device,
        mesh=mesh,
        in_specs=(
            P("band", "dom", None, None),
            P("dom", None, None),
            P(None, "dom", None, None),
            P(),
            P(),
            P(),
            P(),
        ),
        out_specs=(P("band", "dom", None, None), P("band", None)),
        check_vma=False,
    )
```

```python
import jax
import jax.numpy as jnp
import numpy as np
from jax import lax
from jax.experimental import pallas as pl
from jax.experimental.pallas import tpu as pltpu
from jax.sharding import PartitionSpec as P

NY = 64
NCELLS = 196608
PROJ_CELLS = 1000
COEFFS = [
    -5369.0 / 1800.0,
    12.0 / 7.0,
    -15.0 / 56.0,
    10.0 / 189.0,
    -1.0 / 112.0,
    2.0 / 1925.0,
    -1.0 / 16632.0,
]
CENTER = 9.5
HALF = 6.5
KIN = [-0.5 * c for c in COEFFS]
HIGH = lax.Precision.HIGHEST
F32 = jnp.float32


P1_ROWS = 32
P2_ROWS = 40


def place():
    return lax.axis_index("dom"), lax.axis_index("band")


def vmem():
    return pl.BlockSpec(memory_space=pltpu.VMEM)


def smem():
    return pl.BlockSpec(memory_space=pltpu.SMEM)


def params():
    return pltpu.CompilerParams(vmem_limit_bytes=56 * 1024 * 1024)


def pack_kernel(z_ref, x_ref, y_ref, proj_ref, pot_ref, out_ref, pad_ref):
    me, _ = place()
    z_first = (me >> 3) * 6
    x_first = (me & 7) * 8
    pad_ref[:, 24:48, :] = jnp.zeros((64, 24, 128), F32)
    pad_ref[:, 0:24, :] = proj_ref[...]
    lane = lax.broadcasted_iota(jnp.int32, (8, 128), 1)
    sub = lax.broadcasted_iota(jnp.int32, (8, 128), 0)
    slot_lane = lane % 64
    z_cells, x_cells, slots = [], [], []
    for s in range(6):
        row = s + 6 * sub
        z_cells.append(z_first + row // 4)
        x_cells.append(x_first + 2 * (row % 4) + lane // 64)
        slots.append((slot_lane >= 10 * s) & (slot_lane < 10 * s + 10))

    def pair(i, carry):
        for m in range(2):
            a = 2 * i + m
            z0 = z_ref[a]
            x0 = x_ref[a]
            y0 = y_ref[a]
            packed = jnp.zeros((8, 128), F32)
            for s in range(6):
                z, x = z_cells[s], x_cells[s]
                inside = (z >= z0) & (z < z0 + 10) & (x >= x0) & (x < x0 + 10)
                rows = pad_ref[a, pl.ds(s, 8, stride=6), :]
                rows = jnp.where(inside, rows, 0.0)
                rows = pltpu.roll(rows, (128 + 10 * s - y0) & 127, 1)
                packed = jnp.where(slots[s], rows, packed)
            out_ref[i, pl.ds(4 * m, 4), :] = packed[0:4]
        out_ref[i, pl.ds(8, 24), :] = pot_ref[...]
        return carry

    lax.fori_loop(0, 32, pair, 0, unroll=4)


def first_row(z0):
    return (4 * z0 * 171) >> 10


def boxes_kernel(z_ref, got_ref, orb_ref, out_ref, col_ref):
    me, _ = place()
    col_ref[...] = jnp.zeros_like(col_ref)
    for zb in range(8):
        part = got_ref[4 * zb, 0:8, :]
        for q in range(1, 4):
            part = part + got_ref[4 * zb + q, 0:8, :]
        col_ref[0, 4 * zb : 4 * zb + 4, :] = part[0:4]
        col_ref[1, 4 * zb : 4 * zb + 4, :] = part[4:8]
    boxes = []
    for m in range(2):
        z0 = z_ref[2 * (me >> 1) + m]
        boxes.append(col_ref[m, pl.ds(first_row(z0), 8), :])

    def send(n, carry):
        out_ref[n, 0:8, :] = boxes[0]
        out_ref[n, 8:16, :] = boxes[1]
        out_ref[n, 16:40, :] = orb_ref[n]
        return carry

    lax.fori_loop(0, 32, send, 0, unroll=4)


def filter_kernel(
    z_ref, x_ref, y_ref, strength_ref, tapy_ref, tapz_ref, pick_ref, own_ref, oth_ref, ownp_ref, othp_ref, out_ref,
    fld, pot, half, tiles, parts, scaled,
):
    core = place()[0] & 1
    for edge in (slice(0, 3), slice(35, 38)):
        fld[:, edge, :, :] = jnp.zeros((3, 3, 64, 128), F32)
    for edge in (slice(0, 8), slice(56, 64)):
        fld[:, 3:35, edge, :] = jnp.zeros((3, 32, 8, 128), F32)
    for src, src_pot, c in ((own_ref, ownp_ref, core), (oth_ref, othp_ref, 1 - core)):
        for i in range(32):
            zb, q = i // 4, i % 4
            for j in range(4):
                xp = 8 * q + 4 * c + j
                fld[0, 3 + xp, 8 + 6 * zb : 14 + 6 * zb, :] = src.at[i][pl.ds(16 + j, 6, stride=4), :]
                pot[xp, 6 * zb : 6 * zb + 6, :] = src_pot.at[i][pl.ds(8 + j, 6, stride=4), :]

    half[:, pl.ds(pl.multiple_of(8 * core, 8), 8), :] = own_ref[:, 0:16, :].reshape(64, 8, 128)
    half[:, pl.ds(pl.multiple_of(8 - 8 * core, 8), 8), :] = oth_ref[:, 0:16, :].reshape(64, 8, 128)
    slot_lane = lax.broadcasted_iota(jnp.int32, (16, 128), 1) & 63
    in_slot = [(slot_lane >= 10 * n) & (slot_lane < 10 * n + 10) for n in range(6)]

    def expand(a, carry):
        xs = jnp.minimum(x_ref[a] >> 1, 26)
        y0 = y_ref[a]
        z0 = z_ref[a]
        begin = 4 * z0 - 6 * first_row(z0)
        box = half[a]
        moved = [
            pltpu.roll(jnp.where(in_slot[n], box, 0.0), (128 + y0 - 10 * n) & 127, 1) for n in range(6)
        ]
        high, rest = parts_of(jnp.concatenate(moved, axis=0))
        pick = pick_ref[4 * begin + (xs & 7)]
        got = jnp.dot(pick, high, preferred_element_type=F32)
        got = got + jnp.dot(pick, rest, preferred_element_type=F32)
        tiles[pl.ds(6 * a, 6)] = got.reshape(6, 16, 128)
        return carry

    lax.fori_loop(0, 64, expand, 0, unroll=16)

    ones = jnp.ones((128, 128), F32)
    low_half = lax.broadcasted_iota(jnp.int32, (8, 128), 1) < 64
    high_y = tapy_ref[:, 0:128]

    def step(cur, nxt, prev, ca, cb, cg):
        def inner(a, carry):
            xs = jnp.minimum(x_ref[a] >> 1, 26)
            z0 = z_ref[a]
            win = fld[cur, pl.ds(3 + xs, 6), pl.ds(8 + z0, 16), :]
            prod = jnp.sum(win * tiles[pl.ds(6 * a, 6)], axis=0)
            parts[pl.ds(a, 1), :] = jnp.sum(prod, axis=0, keepdims=True)
            return carry

        lax.fori_loop(0, 64, inner, 0, unroll=16)
        sums = jnp.dot(parts[...], ones, precision=HIGH, preferred_element_type=F32)
        scaled[...] = sums

        def along_yz(t, carry):
            rows = fld[cur, pl.ds(3 + 4 * t, 4), 8:56, :]
            high = rows.astype(jnp.bfloat16)
            rest = (rows - high.astype(F32)).astype(jnp.bfloat16)
            flat, flat_rest = high.reshape(192, 128), rest.reshape(192, 128)
            got = jnp.dot(flat, tapy_ref[...], preferred_element_type=F32)
            got = got[:, 0:128] + got[:, 128:256]
            got = got + jnp.dot(flat_rest, high_y, preferred_element_type=F32)
            wide = jnp.concatenate([high[n] for n in range(4)], axis=1)
            wide_rest = jnp.concatenate([rest[n] for n in range(4)], axis=1)
            by_z = jnp.dot(tapz_ref[...], wide, preferred_element_type=F32)
            by_z = by_z[0:48] + by_z[48:96]
            by_z = by_z + jnp.dot(tapz_ref[0:48, :], wide_rest, preferred_element_type=F32)
            for n in range(4):
                fld[nxt, 3 + 4 * t + n, 8:56, :] = got[48 * n : 48 * n + 48] + by_z[:, 128 * n : 128 * n + 128]
            return carry

        lax.fori_loop(0, 8, along_yz, 0, unroll=8)

        def along_x(zt, carry):
            rows = pl.ds(pl.multiple_of(8 + 8 * zt, 8), 8)
            own_rows = pl.ds(pl.multiple_of(8 * zt, 8), 8)
            zero = jnp.zeros((8, 128), F32)
            line = {x: zero for x in (-3, -2, -1, 32, 33, 34, 35)}
            for x in range(3):
                line[x] = fld[cur, 3 + x, rows, :]

            def odd(x):
                total = KIN[1] * (line[x] + line[x - 1]) + KIN[3] * (line[x + 1] + line[x - 2])
                total = total + KIN[5] * (line[x + 2] + line[x - 3])
                return pltpu.roll(total, 64, 1)

            here = odd(0)
            for x in range(32):
                if x + 3 < 32:
                    line[x + 3] = fld[cur, 6 + x, rows, :]
                after = odd(x + 1)
                total = fld[nxt, 3 + x, rows, :] + jnp.where(low_half, here, after)
                total = total + (3.0 * KIN[0] + pot[x, own_rows, :]) * line[x]
                for o in (1, 2, 3):
                    total = total + KIN[2 * o] * (line[x + o] + line[x - o])
                total = ca * total
                if cb != 0.0:
                    total = total + cb * line[x]
                if cg != 0.0:
                    total = total + cg * fld[prev, 3 + x, rows, :]
                fld[nxt, 3 + x, rows, :] = total
                here = after
            return carry

        lax.fori_loop(0, 6, along_x, 0, unroll=2)

        def outer(a, carry):
            xs = jnp.minimum(x_ref[a] >> 1, 26)
            z0 = z_ref[a]
            win = (nxt, pl.ds(3 + xs, 6), pl.ds(8 + z0, 16), slice(None))
            weight = scaled[pl.ds(a, 1), :] * (strength_ref[a] * (ca / PROJ_CELLS))
            fld[win] = fld[win] + weight[None] * tiles[pl.ds(6 * a, 6)]
            return carry

        lax.fori_loop(0, 64, outer, 0, unroll=4)

    def send(which, place):
        for i in range(32):
            zb, q = i // 4, i % 4
            for j in range(4):
                xp = 8 * q + 4 * core + j
                for kh in range(2):
                    z = 8 + 6 * zb + 3 * kh
                    to = ((2 * j + kh) * 32 + i) * 6 + place
                    out_ref[to : to + 3, :] = fld[which, 3 + xp, z : z + 3, :]

    step(0, 1, 2, 1.0 / HALF, -CENTER / HALF, 0.0)
    step(1, 2, 0, 2.0 / HALF, -2.0 * CENTER / HALF, -1.0)
    step(2, 0, 1, 2.0 / HALF, -2.0 * CENTER / HALF, -1.0)
    step(0, 1, 2, 2.0 / HALF, -2.0 * CENTER / HALF, -1.0)
    step(1, 2, 0, 1.0, 0.0, 0.0)
    send(1, 0)
    send(2, 3)


def band_matrix(n, blocks):
    taps = np.zeros((n * blocks, n * blocks), np.float32)
    for b in range(blocks):
        for k in range(n):
            for o in range(1, 7):
                for to in (k - o, k + o):
                    if 0 <= to < n:
                        taps[b * n + k, b * n + to] = KIN[o]
    return taps


def box_rows():
    pick = np.zeros((24, 96, 96), np.float32)
    for begin in (0, 2, 4):
        for first in range(8):
            for w in range(6):
                xp = first + w
                for z in range(10):
                    row, slot = divmod(begin + xp % 4 + 4 * z, 6)
                    pick[4 * begin + first, 16 * w + z, 16 * slot + 8 * (xp // 4 % 2) + row] = 1.0
    return pick


def two_parts(taps, axis):
    high = jnp.asarray(taps).astype(jnp.bfloat16)
    rest = (jnp.asarray(taps) - high.astype(F32)).astype(jnp.bfloat16)
    return jnp.concatenate([high, rest], axis=axis)


def same_core():
    return [[2 * i + c for i in range(32)] for c in range(2)]


def same_core_all():
    return [[(2 * i + c) * 8 + y for y in range(8) for i in range(32)] for c in range(2)]


def near_groups():
    return [
        [(16 * z + 2 * x + c) * 8 + 2 * t + u for x in range(8) for u in range(2)]
        for z in range(4)
        for c in range(2)
        for t in range(4)
    ]


def far_groups():
    return [
        [(16 * z + 2 * x + c) * 8 + 2 * t + u for z in range(4) for t in range(4)]
        for x in range(8)
        for c in range(2)
        for u in range(2)
    ]


def exchange(values, groups):
    return lax.all_to_all(values, ("dom", "band"), 0, 0, tiled=True, axis_index_groups=groups)


def pack(at, proj, pot):
    return pl.pallas_call(
        pack_kernel,
        out_shape=jax.ShapeDtypeStruct((32, P1_ROWS, 128), F32),
        in_specs=[smem()] * 3 + [vmem()] * 2,
        out_specs=vmem(),
        scratch_shapes=[pltpu.VMEM((64, 48, 128), F32)],
        compiler_params=params(),
        name="pack",
    )(*at, proj, pot)


def boxes(at, got, orb):
    return pl.pallas_call(
        boxes_kernel,
        out_shape=jax.ShapeDtypeStruct((32, P2_ROWS, 128), F32),
        in_specs=[smem()] + [vmem()] * 2,
        out_specs=vmem(),
        scratch_shapes=[pltpu.VMEM((2, 40, 128), F32)],
        compiler_params=params(),
        name="boxes",
    )(at[0], got, orb)


def chebyshev(at, strength, own, oth, own_pot, oth_pot):
    tapy = two_parts(band_matrix(NY, 2), 1)
    tapz = two_parts(band_matrix(48, 1), 0)
    return pl.pallas_call(
        filter_kernel,
        out_shape=jax.ShapeDtypeStruct((1536, 128), F32),
        in_specs=[smem()] * 4 + [vmem()] * 7,
        out_specs=vmem(),
        scratch_shapes=[
            pltpu.VMEM((3, 38, 64, 128), F32),
            pltpu.VMEM((32, 48, 128), F32),
            pltpu.VMEM((64, 16, 128), F32),
            pltpu.VMEM((64 * 6, 16, 128), F32),
            pltpu.VMEM((64, 128), F32),
            pltpu.VMEM((64, 128), F32),
        ],
        compiler_params=params(),
        name="chebyshev",
    )(*at, strength, tapy, tapz, jnp.asarray(box_rows(), jnp.bfloat16), own, oth, own_pot, oth_pot)


def dot(a, b):
    return jnp.dot(a, b, precision=HIGH, preferred_element_type=F32)


def dot_t(a, b):
    return lax.dot_general(a, b, (((1,), (1,)), ((), ())), precision=HIGH, preferred_element_type=F32)


def parts_of(a):
    high = a.astype(jnp.bfloat16)
    return high, (a - high.astype(F32)).astype(jnp.bfloat16)


def dot_parts(a, b, turn=False):
    dims = (((1,), (1 if turn else 0,)), ((), ()))
    (ah, ar), (bh, br) = a, b
    total = lax.dot_general(ah, br, dims, preferred_element_type=F32)
    total = total + lax.dot_general(ar, bh, dims, preferred_element_type=F32)
    return total + lax.dot_general(ah, bh, dims, preferred_element_type=F32)


def gram_kernel(both_ref, mine_ref, other_ref):
    core = place()[0] & 1
    f = jnp.concatenate([both_ref[pl.ds(r, 256, stride=6), :] for r in range(3)], axis=1)
    g = jnp.concatenate([both_ref[pl.ds(3 + r, 256, stride=6), :] for r in range(3)], axis=1)
    f = parts_of(f)
    corr = dot_parts(f, f, True)
    ham = dot_parts(f, parts_of(g), True)
    row = lax.broadcasted_iota(jnp.int32, (256, 256), 0)
    col = lax.broadcasted_iota(jnp.int32, (256, 256), 1)
    packed = jnp.where(row >= col, corr, ham)
    diag = jnp.sum(jnp.where(row == col, ham, 0.0), axis=0, keepdims=True)
    for ref, first in ((mine_ref, core == 0), (other_ref, core == 1)):
        half = jnp.where(first, packed[:, 0:128], packed[:, 128:256])
        for q in range(16):
            ref[q, 0:16, :] = half[16 * q : 16 * q + 16]
            ref[q, 16:24, :] = jnp.zeros((8, 128), F32)
        ref[0, 16:17, :] = jnp.where(first, diag[:, 0:128], diag[:, 128:256])


def ortho_kernel(own_ref, oth_ref, both_ref, rot_ref, proj_ref, corr, ham, inv, work):
    me, block = place()
    core = me & 1
    row = lax.broadcasted_iota(jnp.int32, (256, 256), 0)
    col = lax.broadcasted_iota(jnp.int32, (256, 256), 1)
    below = row > col
    same = row == col
    scale = 1.0 / NCELLS
    diag = []
    for h in range(2):
        for q in range(16):
            half = jnp.where(core == h, own_ref[q, 0:16, :], oth_ref[q, 0:16, :])
            work[16 * q : 16 * q + 16, 128 * h : 128 * h + 128] = half
        diag.append(jnp.where(core == h, own_ref[0, 16:17, :], oth_ref[0, 16:17, :]))
    packed = work[...] * scale
    turned = packed.T
    diag = jnp.concatenate(diag, axis=1) * scale
    corr[...] = jnp.where(row >= col, packed, turned)
    ham[...] = jnp.where(same, diag, jnp.where(below, turned, packed))

    def half_lower(e):
        return jnp.where(below, e, jnp.where(same, 0.5 * e, 0.0))

    own = jnp.where(same, corr[...], 0.0)
    by_col = lax.rsqrt(jnp.sum(own, axis=0, keepdims=True))
    by_row = lax.rsqrt(jnp.sum(own, axis=1, keepdims=True))
    first = half_lower(by_row * corr[...] * by_col - jnp.where(same, 1.0, 0.0))
    inv[...] = jnp.where(same, by_col, 0.0) - first * by_col

    def rough(a, b, turn=False):
        dims = (((1,), (1 if turn else 0,)), ((), ()))
        return lax.dot_general(
            a.astype(jnp.bfloat16), b.astype(jnp.bfloat16), dims, preferred_element_type=F32
        )

    for _ in range(2):
        x = inv[...]
        e = rough(rough(x, corr[...]), x, True) - jnp.where(same, 1.0, 0.0)
        inv[...] = x - rough(half_lower(e), x)

    def refine(state):
        count, _ = state
        x = inv[...]
        e = dot_t(dot(x, corr[...]), x) - jnp.where(same, 1.0, 0.0)
        inv[...] = x - dot(half_lower(e), x)
        return count + 1, jnp.sum(e * e)

    def going(state):
        count, size = state
        return (count < 8) & jnp.logical_not(size < 1e-6)

    _, size = lax.while_loop(going, refine, (jnp.int32(0), jnp.float32(1.0)))
    least = jnp.min(jnp.where(same, inv[...], 1.0))

    @pl.when(jnp.logical_not((size < 1e-6) & (least > 0.0)))
    def _():
        work[...] = corr[...]
        inv[...] = jnp.where(same, 1.0, 0.0)

        def column(j, carry):
            picked = jnp.sum(jnp.where(col == j, work[...], 0.0), axis=1, keepdims=True)
            at_j = lax.broadcasted_iota(jnp.int32, (256, 1), 0)
            pivot = jnp.sum(jnp.where(at_j == j, picked, 0.0), axis=0, keepdims=True)
            factor = 1.0 / jnp.sqrt(pivot)
            inv[pl.ds(j, 1), :] = inv[pl.ds(j, 1), :] * factor
            down = jnp.where(at_j > j, picked, 0.0) * factor
            work[...] = work[...] - down * (work[pl.ds(j, 1), :] * factor)
            inv[...] = inv[...] - down * inv[pl.ds(j, 1), :]
            return carry

        lax.fori_loop(0, 256, column, 0)

    x = inv[...]
    mine = inv[pl.ds(pl.multiple_of(32 * block, 32), 32), :]
    proj_ref[...] = dot_t(dot(mine, ham[...]), x)
    f = jnp.concatenate([both_ref[pl.ds(r, 256, stride=6), :] for r in range(3)], axis=1)
    turned = dot_parts(parts_of(x), parts_of(f))
    for r in range(3):
        rot_ref[pl.ds(r, 256, stride=3), :] = turned[:, 128 * r : 128 * r + 128]


def gram(both):
    return pl.pallas_call(
        gram_kernel,
        out_shape=[jax.ShapeDtypeStruct((16, 24, 128), F32)] * 2,
        in_specs=[vmem()],
        out_specs=[vmem()] * 2,
        compiler_params=params(),
        name="gram",
    )(both)


def ortho(own, oth, both):
    return pl.pallas_call(
        ortho_kernel,
        out_shape=[jax.ShapeDtypeStruct((768, 128), F32), jax.ShapeDtypeStruct((32, 256), F32)],
        in_specs=[vmem()] * 3,
        out_specs=[vmem()] * 2,
        scratch_shapes=[pltpu.VMEM((256, 256), F32)] * 4,
        compiler_params=params(),
        name="ortho",
    )(own, oth, both)


def swap_cores(values):
    return lax.ppermute(values, "dom", [(i, i ^ 1) for i in range(64)])


def sum_everywhere(values):
    for groups in (near_groups(), far_groups()):
        part = jnp.sum(exchange(values, groups), axis=0)
        values = jnp.broadcast_to(part[None], values.shape)
    return exchange(values, near_groups())


def on_device(orbitals, potential, proj_shape, proj_strength, atom_z, atom_x, atom_y):
    at = (atom_z, atom_x, atom_y)
    first = pack(at, proj_shape.reshape(64, 24, 128), potential.reshape(24, 128))
    first = lax.all_to_all(first, "dom", 0, 0, tiled=True, axis_index_groups=same_core())
    first_oth = swap_cores(first)
    second = boxes(at, first, orbitals.reshape(32, 24, 128))
    second = lax.all_to_all(second, "dom", 0, 0, tiled=True, axis_index_groups=same_core())
    second_oth = swap_cores(second)
    both = chebyshev(at, proj_strength, second, second_oth, first, first_oth)
    both = both.reshape(256, 3, 2, 128)
    both = exchange(both, same_core_all())
    both = both.reshape(1536, 128)
    mine, other = gram(both)
    mine = sum_everywhere(mine + swap_cores(other))
    rotated, projected = ortho(mine, swap_cores(mine), both)
    rotated = lax.all_to_all(rotated.reshape(8, 96, 128), "band", 0, 0, tiled=True)
    rotated = rotated.reshape(4, 2, 32, 3, 128).transpose(2, 1, 3, 0, 4)
    return (rotated.reshape(32, 1, 6, 512), projected)


def solution(mesh):
    return jax.shard_map(
        on_device,
        mesh=mesh,
        in_specs=(
            P("band", "dom", None, None),
            P("dom", None, None),
            P(None, "dom", None, None),
            P(),
            P(),
            P(),
            P(),
        ),
        out_specs=(P("band", "dom", None, None), P("band", None)),
        check_vma=False,
    )
```

```python
import jax
import jax.numpy as jnp
import numpy as np
from jax import lax
from jax.experimental import pallas as pl
from jax.experimental.pallas import tpu as pltpu
from jax.sharding import PartitionSpec as P

NY = 64
NCELLS = 196608
PROJ_CELLS = 1000
COEFFS = [
    -5369.0 / 1800.0,
    12.0 / 7.0,
    -15.0 / 56.0,
    10.0 / 189.0,
    -1.0 / 112.0,
    2.0 / 1925.0,
    -1.0 / 16632.0,
]
CENTER = 9.5
HALF = 6.5
KIN = [-0.5 * c for c in COEFFS]
HIGH = lax.Precision.HIGHEST
F32 = jnp.float32


P1_ROWS = 32
P2_ROWS = 40


def place():
    return lax.axis_index("dom"), lax.axis_index("band")


def vmem():
    return pl.BlockSpec(memory_space=pltpu.VMEM)


def smem():
    return pl.BlockSpec(memory_space=pltpu.SMEM)


def params(megabytes):
    return pltpu.CompilerParams(vmem_limit_bytes=megabytes * 1024 * 1024)


def pack_kernel(z_ref, x_ref, y_ref, proj_ref, pot_ref, out_ref, pad_ref):
    me, _ = place()
    z_first = (me >> 3) * 6
    x_first = (me & 7) * 8
    pad_ref[:, 24:48, :] = jnp.zeros((64, 24, 128), F32)
    pad_ref[:, 0:24, :] = proj_ref[...]
    lane = lax.broadcasted_iota(jnp.int32, (8, 128), 1)
    sub = lax.broadcasted_iota(jnp.int32, (8, 128), 0)
    slot_lane = lane % 64
    z_cells, x_cells, slots = [], [], []
    for s in range(6):
        row = s + 6 * sub
        z_cells.append(z_first + row // 4)
        x_cells.append(x_first + 2 * (row % 4) + lane // 64)
        slots.append((slot_lane >= 10 * s) & (slot_lane < 10 * s + 10))

    def pair(i, carry):
        for m in range(2):
            a = 2 * i + m
            z0 = z_ref[a]
            x0 = x_ref[a]
            y0 = y_ref[a]
            packed = jnp.zeros((8, 128), F32)
            for s in range(6):
                z, x = z_cells[s], x_cells[s]
                inside = (z >= z0) & (z < z0 + 10) & (x >= x0) & (x < x0 + 10)
                rows = pad_ref[a, pl.ds(s, 8, stride=6), :]
                rows = jnp.where(inside, rows, 0.0)
                rows = pltpu.roll(rows, (128 + 10 * s - y0) & 127, 1)
                packed = jnp.where(slots[s], rows, packed)
            out_ref[i, pl.ds(4 * m, 4), :] = packed[0:4]
        out_ref[i, pl.ds(8, 24), :] = pot_ref[...]
        return carry

    lax.fori_loop(0, 32, pair, 0, unroll=4)


def first_row(z0):
    return (4 * z0 * 171) >> 10


def boxes_kernel(z_ref, got_ref, orb_ref, out_ref, col_ref):
    me, _ = place()
    col_ref[...] = jnp.zeros_like(col_ref)
    for zb in range(8):
        part = got_ref[4 * zb, 0:8, :]
        for q in range(1, 4):
            part = part + got_ref[4 * zb + q, 0:8, :]
        col_ref[0, 4 * zb : 4 * zb + 4, :] = part[0:4]
        col_ref[1, 4 * zb : 4 * zb + 4, :] = part[4:8]
    boxes = []
    for m in range(2):
        z0 = z_ref[2 * (me >> 1) + m]
        boxes.append(col_ref[m, pl.ds(first_row(z0), 8), :])

    def send(n, carry):
        out_ref[n, 0:8, :] = boxes[0]
        out_ref[n, 8:16, :] = boxes[1]
        out_ref[n, 16:40, :] = orb_ref[n]
        return carry

    lax.fori_loop(0, 32, send, 0, unroll=4)


def filter_kernel(
    z_ref, x_ref, y_ref, strength_ref, tapy_ref, tapz_ref, pick_ref, own_ref, oth_ref, ownp_ref, othp_ref, out_ref,
    fld, pot, half, tiles, parts, scaled,
):
    core = place()[0] & 1
    for edge in (slice(0, 3), slice(35, 38)):
        fld[:, edge, :, :] = jnp.zeros((3, 3, 64, 128), F32)
    for edge in (slice(0, 8), slice(56, 64)):
        fld[:, 3:35, edge, :] = jnp.zeros((3, 32, 8, 128), F32)
    for src, src_pot, c in ((own_ref, ownp_ref, core), (oth_ref, othp_ref, 1 - core)):
        for i in range(32):
            zb, q = i // 4, i % 4
            for j in range(4):
                xp = 8 * q + 4 * c + j
                fld[0, 3 + xp, 8 + 6 * zb : 14 + 6 * zb, :] = src.at[i][pl.ds(16 + j, 6, stride=4), :]
                pot[xp, 6 * zb : 6 * zb + 6, :] = src_pot.at[i][pl.ds(8 + j, 6, stride=4), :]

    half[:, pl.ds(pl.multiple_of(8 * core, 8), 8), :] = own_ref[:, 0:16, :].reshape(64, 8, 128)
    half[:, pl.ds(pl.multiple_of(8 - 8 * core, 8), 8), :] = oth_ref[:, 0:16, :].reshape(64, 8, 128)
    slot_lane = lax.broadcasted_iota(jnp.int32, (16, 128), 1) & 63
    in_slot = [(slot_lane >= 10 * n) & (slot_lane < 10 * n + 10) for n in range(6)]

    def expand(a, carry):
        xs = jnp.minimum(x_ref[a] >> 1, 26)
        y0 = y_ref[a]
        z0 = z_ref[a]
        begin = 4 * z0 - 6 * first_row(z0)
        box = half[a]
        moved = [
            pltpu.roll(jnp.where(in_slot[n], box, 0.0), (128 + y0 - 10 * n) & 127, 1) for n in range(6)
        ]
        high, rest = parts_of(jnp.concatenate(moved, axis=0))
        pick = pick_ref[4 * begin + (xs & 7)]
        got = jnp.dot(pick, high, preferred_element_type=F32)
        got = got + jnp.dot(pick, rest, preferred_element_type=F32)
        tiles[pl.ds(6 * a, 6)] = got.reshape(6, 16, 128)
        return carry

    lax.fori_loop(0, 64, expand, 0, unroll=16)

    ones = jnp.ones((128, 128), F32)
    low_half = lax.broadcasted_iota(jnp.int32, (8, 128), 1) < 64
    high_y = tapy_ref[:, 0:128]

    def step(cur, nxt, prev, ca, cb, cg):
        def inner(a, carry):
            xs = jnp.minimum(x_ref[a] >> 1, 26)
            z0 = z_ref[a]
            win = fld[cur, pl.ds(3 + xs, 6), pl.ds(8 + z0, 16), :]
            prod = jnp.sum(win * tiles[pl.ds(6 * a, 6)], axis=0)
            parts[pl.ds(a, 1), :] = jnp.sum(prod, axis=0, keepdims=True)
            return carry

        lax.fori_loop(0, 64, inner, 0, unroll=16)
        sums = jnp.dot(parts[...], ones, precision=HIGH, preferred_element_type=F32)
        scaled[...] = sums

        def along_yz(t, carry):
            rows = fld[cur, pl.ds(3 + 4 * t, 4), 8:56, :]
            high = rows.astype(jnp.bfloat16)
            rest = (rows - high.astype(F32)).astype(jnp.bfloat16)
            flat, flat_rest = high.reshape(192, 128), rest.reshape(192, 128)
            got = jnp.dot(flat, tapy_ref[...], preferred_element_type=F32)
            got = got[:, 0:128] + got[:, 128:256]
            got = got + jnp.dot(flat_rest, high_y, preferred_element_type=F32)
            wide = jnp.concatenate([high[n] for n in range(4)], axis=1)
            wide_rest = jnp.concatenate([rest[n] for n in range(4)], axis=1)
            by_z = jnp.dot(tapz_ref[...], wide, preferred_element_type=F32)
            by_z = by_z[0:48] + by_z[48:96]
            by_z = by_z + jnp.dot(tapz_ref[0:48, :], wide_rest, preferred_element_type=F32)
            for n in range(4):
                fld[nxt, 3 + 4 * t + n, 8:56, :] = got[48 * n : 48 * n + 48] + by_z[:, 128 * n : 128 * n + 128]
            return carry

        lax.fori_loop(0, 8, along_yz, 0, unroll=8)

        def along_x(zt, carry):
            rows = pl.ds(pl.multiple_of(8 + 8 * zt, 8), 8)
            own_rows = pl.ds(pl.multiple_of(8 * zt, 8), 8)
            zero = jnp.zeros((8, 128), F32)
            line = {x: zero for x in (-3, -2, -1, 32, 33, 34, 35)}
            for x in range(3):
                line[x] = fld[cur, 3 + x, rows, :]

            def odd(x):
                total = KIN[1] * (line[x] + line[x - 1]) + KIN[3] * (line[x + 1] + line[x - 2])
                total = total + KIN[5] * (line[x + 2] + line[x - 3])
                return pltpu.roll(total, 64, 1)

            here = odd(0)
            for x in range(32):
                if x + 3 < 32:
                    line[x + 3] = fld[cur, 6 + x, rows, :]
                after = odd(x + 1)
                total = fld[nxt, 3 + x, rows, :] + jnp.where(low_half, here, after)
                total = total + (3.0 * KIN[0] + pot[x, own_rows, :]) * line[x]
                for o in (1, 2, 3):
                    total = total + KIN[2 * o] * (line[x + o] + line[x - o])
                total = ca * total
                if cb != 0.0:
                    total = total + cb * line[x]
                if cg != 0.0:
                    total = total + cg * fld[prev, 3 + x, rows, :]
                fld[nxt, 3 + x, rows, :] = total
                here = after
            return carry

        lax.fori_loop(0, 6, along_x, 0, unroll=2)

        def outer(a, carry):
            xs = jnp.minimum(x_ref[a] >> 1, 26)
            z0 = z_ref[a]
            win = (nxt, pl.ds(3 + xs, 6), pl.ds(8 + z0, 16), slice(None))
            weight = scaled[pl.ds(a, 1), :] * (strength_ref[a] * (ca / PROJ_CELLS))
            fld[win] = fld[win] + weight[None] * tiles[pl.ds(6 * a, 6)]
            return carry

        lax.fori_loop(0, 64, outer, 0, unroll=4)

    def send(which, place):
        for i in range(32):
            zb, q = i // 4, i % 4
            for j in range(4):
                xp = 8 * q + 4 * core + j
                for kh in range(2):
                    z = 8 + 6 * zb + 3 * kh
                    to = ((2 * j + kh) * 32 + i) * 6 + place
                    out_ref[to : to + 3, :] = fld[which, 3 + xp, z : z + 3, :]

    step(0, 1, 2, 1.0 / HALF, -CENTER / HALF, 0.0)
    step(1, 2, 0, 2.0 / HALF, -2.0 * CENTER / HALF, -1.0)
    step(2, 0, 1, 2.0 / HALF, -2.0 * CENTER / HALF, -1.0)
    step(0, 1, 2, 2.0 / HALF, -2.0 * CENTER / HALF, -1.0)
    step(1, 2, 0, 1.0, 0.0, 0.0)
    send(1, 0)
    send(2, 3)


def band_matrix(n, blocks):
    taps = np.zeros((n * blocks, n * blocks), np.float32)
    for b in range(blocks):
        for k in range(n):
            for o in range(1, 7):
                for to in (k - o, k + o):
                    if 0 <= to < n:
                        taps[b * n + k, b * n + to] = KIN[o]
    return taps


def box_rows():
    pick = np.zeros((24, 96, 96), np.float32)
    for begin in (0, 2, 4):
        for first in range(8):
            for w in range(6):
                xp = first + w
                for z in range(10):
                    row, slot = divmod(begin + xp % 4 + 4 * z, 6)
                    pick[4 * begin + first, 16 * w + z, 16 * slot + 8 * (xp // 4 % 2) + row] = 1.0
    return pick


def two_parts(taps, axis):
    high = jnp.asarray(taps).astype(jnp.bfloat16)
    rest = (jnp.asarray(taps) - high.astype(F32)).astype(jnp.bfloat16)
    return jnp.concatenate([high, rest], axis=axis)


def same_core():
    return [[2 * i + c for i in range(32)] for c in range(2)]


def same_core_all():
    return [[(2 * i + c) * 8 + y for y in range(8) for i in range(32)] for c in range(2)]


def near_groups():
    return [
        [(16 * z + 2 * x + c) * 8 + 2 * t + u for x in range(8) for u in range(2)]
        for z in range(4)
        for c in range(2)
        for t in range(4)
    ]


def far_groups():
    return [
        [(16 * z + 2 * x + c) * 8 + 2 * t + u for z in range(4) for t in range(4)]
        for x in range(8)
        for c in range(2)
        for u in range(2)
    ]


def exchange(values, groups):
    return lax.all_to_all(values, ("dom", "band"), 0, 0, tiled=True, axis_index_groups=groups)


def pack(at, proj, pot):
    return pl.pallas_call(
        pack_kernel,
        out_shape=jax.ShapeDtypeStruct((32, P1_ROWS, 128), F32),
        in_specs=[smem()] * 3 + [vmem()] * 2,
        out_specs=vmem(),
        scratch_shapes=[pltpu.VMEM((64, 48, 128), F32)],
        compiler_params=params(8),
        name="pack",
    )(*at, proj, pot)


def boxes(at, got, orb):
    return pl.pallas_call(
        boxes_kernel,
        out_shape=jax.ShapeDtypeStruct((32, P2_ROWS, 128), F32),
        in_specs=[smem()] + [vmem()] * 2,
        out_specs=vmem(),
        scratch_shapes=[pltpu.VMEM((2, 40, 128), F32)],
        compiler_params=params(6),
        name="boxes",
    )(at[0], got, orb)


def chebyshev(at, strength, own, oth, own_pot, oth_pot):
    tapy = two_parts(band_matrix(NY, 2), 1)
    tapz = two_parts(band_matrix(48, 1), 0)
    return pl.pallas_call(
        filter_kernel,
        out_shape=jax.ShapeDtypeStruct((1536, 128), F32),
        in_specs=[smem()] * 4 + [vmem()] * 7,
        out_specs=vmem(),
        scratch_shapes=[
            pltpu.VMEM((3, 38, 64, 128), F32),
            pltpu.VMEM((32, 48, 128), F32),
            pltpu.VMEM((64, 16, 128), F32),
            pltpu.VMEM((64 * 6, 16, 128), F32),
            pltpu.VMEM((64, 128), F32),
            pltpu.VMEM((64, 128), F32),
        ],
        compiler_params=params(24),
        name="chebyshev",
    )(*at, strength, tapy, tapz, jnp.asarray(box_rows(), jnp.bfloat16), own, oth, own_pot, oth_pot)


def dot(a, b):
    return jnp.dot(a, b, precision=HIGH, preferred_element_type=F32)


def dot_t(a, b):
    return lax.dot_general(a, b, (((1,), (1,)), ((), ())), precision=HIGH, preferred_element_type=F32)


def parts_of(a):
    high = a.astype(jnp.bfloat16)
    return high, (a - high.astype(F32)).astype(jnp.bfloat16)


def dot_parts(a, b, turn=False):
    dims = (((1,), (1 if turn else 0,)), ((), ()))
    (ah, ar), (bh, br) = a, b
    total = lax.dot_general(ah, br, dims, preferred_element_type=F32)
    total = total + lax.dot_general(ar, bh, dims, preferred_element_type=F32)
    return total + lax.dot_general(ah, bh, dims, preferred_element_type=F32)


def gram_kernel(both_ref, mine_ref, other_ref, f_ref):
    core = place()[0] & 1
    f = [both_ref[pl.ds(r, 256, stride=6), :] for r in range(3)]
    for r in range(3):
        f_ref[r] = f[r]
    f = jnp.concatenate(f, axis=1)
    g = jnp.concatenate([both_ref[pl.ds(3 + r, 256, stride=6), :] for r in range(3)], axis=1)
    f = parts_of(f)
    corr = dot_parts(f, f, True)
    ham = dot_parts(f, parts_of(g), True)
    row = lax.broadcasted_iota(jnp.int32, (256, 256), 0)
    col = lax.broadcasted_iota(jnp.int32, (256, 256), 1)
    packed = jnp.where(row >= col, corr, ham)
    diag = jnp.sum(jnp.where(row == col, ham, 0.0), axis=0, keepdims=True)
    for ref, first in ((mine_ref, core == 0), (other_ref, core == 1)):
        half = jnp.where(first, packed[:, 0:128], packed[:, 128:256])
        for q in range(16):
            ref[q, 0:16, :] = half[16 * q : 16 * q + 16]
            ref[q, 16:24, :] = jnp.zeros((8, 128), F32)
        ref[0, 16:17, :] = jnp.where(first, diag[:, 0:128], diag[:, 128:256])


def ortho_kernel(own_ref, oth_ref, rows_ref, proj_ref, corr, ham, inv, work):
    me, block = place()
    core = me & 1
    row = lax.broadcasted_iota(jnp.int32, (256, 256), 0)
    col = lax.broadcasted_iota(jnp.int32, (256, 256), 1)
    below = row > col
    same = row == col
    scale = 1.0 / NCELLS
    diag = []
    for h in range(2):
        for q in range(16):
            half = jnp.where(core == h, own_ref[q, 0:16, :], oth_ref[q, 0:16, :])
            work[16 * q : 16 * q + 16, 128 * h : 128 * h + 128] = half
        diag.append(jnp.where(core == h, own_ref[0, 16:17, :], oth_ref[0, 16:17, :]))
    packed = work[...] * scale
    turned = packed.T
    diag = jnp.concatenate(diag, axis=1) * scale
    corr[...] = jnp.where(row >= col, packed, turned)
    ham[...] = jnp.where(same, diag, jnp.where(below, turned, packed))

    def half_lower(e):
        return jnp.where(below, e, jnp.where(same, 0.5 * e, 0.0))

    own = jnp.where(same, corr[...], 0.0)
    by_col = lax.rsqrt(jnp.sum(own, axis=0, keepdims=True))
    by_row = lax.rsqrt(jnp.sum(own, axis=1, keepdims=True))
    first = half_lower(by_row * corr[...] * by_col - jnp.where(same, 1.0, 0.0))
    inv[...] = jnp.where(same, by_col, 0.0) - first * by_col

    def rough(a, b, turn=False):
        dims = (((1,), (1 if turn else 0,)), ((), ()))
        return lax.dot_general(
            a.astype(jnp.bfloat16), b.astype(jnp.bfloat16), dims, preferred_element_type=F32
        )

    for _ in range(2):
        x = inv[...]
        e = rough(rough(x, corr[...]), x, True) - jnp.where(same, 1.0, 0.0)
        inv[...] = x - rough(half_lower(e), x)

    def refine(state):
        count, _ = state
        x = inv[...]
        e = dot_t(dot(x, corr[...]), x) - jnp.where(same, 1.0, 0.0)
        inv[...] = x - dot(half_lower(e), x)
        return count + 1, jnp.sum(e * e)

    def going(state):
        count, size = state
        return (count < 8) & jnp.logical_not(size < 1e-6)

    _, size = lax.while_loop(going, refine, (jnp.int32(0), jnp.float32(1.0)))
    least = jnp.min(jnp.where(same, inv[...], 1.0))

    @pl.when(jnp.logical_not((size < 1e-6) & (least > 0.0)))
    def _():
        work[...] = corr[...]
        inv[...] = jnp.where(same, 1.0, 0.0)

        def column(j, carry):
            picked = jnp.sum(jnp.where(col == j, work[...], 0.0), axis=1, keepdims=True)
            at_j = lax.broadcasted_iota(jnp.int32, (256, 1), 0)
            pivot = jnp.sum(jnp.where(at_j == j, picked, 0.0), axis=0, keepdims=True)
            factor = 1.0 / jnp.sqrt(pivot)
            inv[pl.ds(j, 1), :] = inv[pl.ds(j, 1), :] * factor
            down = jnp.where(at_j > j, picked, 0.0) * factor
            work[...] = work[...] - down * (work[pl.ds(j, 1), :] * factor)
            inv[...] = inv[...] - down * inv[pl.ds(j, 1), :]
            return carry

        lax.fori_loop(0, 256, column, 0)

    x = inv[...]
    mine = inv[pl.ds(pl.multiple_of(32 * block, 32), 32), :]
    proj_ref[...] = dot_t(dot(mine, ham[...]), x)
    rows_ref[...] = mine


def rotate_kernel(rows_ref, all_ref, out_ref):
    rows = parts_of(rows_ref[...])
    for part in range(8):
        j, kh = part // 2, part % 2
        f = jnp.concatenate([all_ref[3 * part + t] for t in range(3)], axis=1)
        turned = dot_parts(rows, parts_of(f))
        for t in range(3):
            out_ref[pl.ds((3 * kh + t) * 4 + j, 32, stride=24), :] = turned[:, 128 * t : 128 * t + 128]


def gram(both):
    return pl.pallas_call(
        gram_kernel,
        out_shape=[jax.ShapeDtypeStruct((16, 24, 128), F32)] * 2 + [jax.ShapeDtypeStruct((3, 256, 128), F32)],
        in_specs=[vmem()],
        out_specs=[vmem()] * 3,
        compiler_params=params(8),
        name="gram",
    )(both)


def ortho(own, oth):
    return pl.pallas_call(
        ortho_kernel,
        out_shape=[jax.ShapeDtypeStruct((32, 256), F32)] * 2,
        in_specs=[vmem()] * 2,
        out_specs=[vmem()] * 2,
        scratch_shapes=[pltpu.VMEM((256, 256), F32)] * 4,
        compiler_params=params(8),
        name="ortho",
    )(own, oth)


def rotate(rows, every):
    return pl.pallas_call(
        rotate_kernel,
        out_shape=jax.ShapeDtypeStruct((768, 128), F32),
        in_specs=[vmem()] * 2,
        out_specs=vmem(),
        compiler_params=params(12),
        name="rotate",
    )(rows, every)


def swap_cores(values):
    return lax.ppermute(values, "dom", [(i, i ^ 1) for i in range(64)])


def sum_everywhere(values):
    for groups in (near_groups(), far_groups()):
        part = jnp.sum(exchange(values, groups), axis=0)
        values = jnp.broadcast_to(part[None], values.shape)
    return exchange(values, near_groups())


def on_device(orbitals, potential, proj_shape, proj_strength, atom_z, atom_x, atom_y):
    at = (atom_z, atom_x, atom_y)
    first = pack(at, proj_shape.reshape(64, 24, 128), potential.reshape(24, 128))
    first = lax.all_to_all(first, "dom", 0, 0, tiled=True, axis_index_groups=same_core())
    first_oth = swap_cores(first)
    second = boxes(at, first, orbitals.reshape(32, 24, 128))
    second = lax.all_to_all(second, "dom", 0, 0, tiled=True, axis_index_groups=same_core())
    second_oth = swap_cores(second)
    both = chebyshev(at, proj_strength, second, second_oth, first, first_oth)
    both = both.reshape(256, 3, 2, 128)
    both = exchange(both, same_core_all())
    both = both.reshape(1536, 128)
    mine, other, filtered = gram(both)
    every = lax.all_gather(filtered, "band", axis=0, tiled=True)
    mine = sum_everywhere(mine + swap_cores(other))
    rows, projected = ortho(mine, swap_cores(mine))
    rotated = rotate(rows, every)
    return (rotated.reshape(32, 1, 6, 512), projected)


def solution(mesh):
    return jax.shard_map(
        on_device,
        mesh=mesh,
        in_specs=(
            P("band", "dom", None, None),
            P("dom", None, None),
            P(None, "dom", None, None),
            P(),
            P(),
            P(),
            P(),
        ),
        out_specs=(P("band", "dom", None, None), P("band", None)),
        check_vma=False,
    )
```

```python
import jax
import jax.numpy as jnp
import numpy as np
from jax import lax
from jax.experimental import pallas as pl
from jax.experimental.pallas import tpu as pltpu
from jax.sharding import PartitionSpec as P

NY = 64
NCELLS = 196608
PROJ_CELLS = 1000
COEFFS = [
    -5369.0 / 1800.0,
    12.0 / 7.0,
    -15.0 / 56.0,
    10.0 / 189.0,
    -1.0 / 112.0,
    2.0 / 1925.0,
    -1.0 / 16632.0,
]
CENTER = 9.5
HALF = 6.5
KIN = [-0.5 * c for c in COEFFS]
HIGH = lax.Precision.HIGHEST
F32 = jnp.float32


P1_ROWS = 32
P2_ROWS = 40


def place():
    return lax.axis_index("dom"), lax.axis_index("band")


def vmem():
    return pl.BlockSpec(memory_space=pltpu.VMEM)


def smem():
    return pl.BlockSpec(memory_space=pltpu.SMEM)


def params(megabytes):
    return pltpu.CompilerParams(vmem_limit_bytes=megabytes * 1024 * 1024)


def pack_kernel(z_ref, x_ref, y_ref, proj_ref, pot_ref, out_ref, pad_ref):
    me, _ = place()
    z_first = (me >> 3) * 6
    x_first = (me & 7) * 8
    pad_ref[:, 24:48, :] = jnp.zeros((64, 24, 128), F32)
    pad_ref[:, 0:24, :] = proj_ref[...]
    lane = lax.broadcasted_iota(jnp.int32, (8, 128), 1)
    sub = lax.broadcasted_iota(jnp.int32, (8, 128), 0)
    slot_lane = lane % 64
    z_cells, x_cells, slots = [], [], []
    for s in range(6):
        row = s + 6 * sub
        z_cells.append(z_first + row // 4)
        x_cells.append(x_first + 2 * (row % 4) + lane // 64)
        slots.append((slot_lane >= 10 * s) & (slot_lane < 10 * s + 10))

    def pair(i, carry):
        for m in range(2):
            a = 2 * i + m
            z0 = z_ref[a]
            x0 = x_ref[a]
            y0 = y_ref[a]
            packed = jnp.zeros((8, 128), F32)
            for s in range(6):
                z, x = z_cells[s], x_cells[s]
                inside = (z >= z0) & (z < z0 + 10) & (x >= x0) & (x < x0 + 10)
                rows = pad_ref[a, pl.ds(s, 8, stride=6), :]
                rows = jnp.where(inside, rows, 0.0)
                rows = pltpu.roll(rows, (128 + 10 * s - y0) & 127, 1)
                packed = jnp.where(slots[s], rows, packed)
            out_ref[i, pl.ds(4 * m, 4), :] = packed[0:4]
        out_ref[i, pl.ds(8, 24), :] = pot_ref[...]
        return carry

    lax.fori_loop(0, 32, pair, 0, unroll=4)


def first_row(z0):
    return (4 * z0 * 171) >> 10


def boxes_kernel(z_ref, got_ref, orb_ref, out_ref, col_ref):
    me, _ = place()
    col_ref[...] = jnp.zeros_like(col_ref)
    for zb in range(8):
        part = got_ref[4 * zb, 0:8, :]
        for q in range(1, 4):
            part = part + got_ref[4 * zb + q, 0:8, :]
        col_ref[0, 4 * zb : 4 * zb + 4, :] = part[0:4]
        col_ref[1, 4 * zb : 4 * zb + 4, :] = part[4:8]
    boxes = []
    for m in range(2):
        z0 = z_ref[2 * (me >> 1) + m]
        boxes.append(col_ref[m, pl.ds(first_row(z0), 8), :])

    def send(n, carry):
        out_ref[n, 0:8, :] = boxes[0]
        out_ref[n, 8:16, :] = boxes[1]
        out_ref[n, 16:40, :] = orb_ref[n]
        return carry

    lax.fori_loop(0, 32, send, 0, unroll=4)


def filter_kernel(
    z_ref, x_ref, y_ref, strength_ref, tapy_ref, tapz_ref, pick_ref, own_ref, oth_ref, ownp_ref, othp_ref, out_ref,
    fld, pot, half, tiles, parts, scaled,
):
    core = place()[0] & 1
    for edge in (slice(0, 3), slice(35, 38)):
        fld[:, edge, :, :] = jnp.zeros((3, 3, 64, 128), F32)
    for edge in (slice(0, 8), slice(56, 64)):
        fld[:, 3:35, edge, :] = jnp.zeros((3, 32, 8, 128), F32)
    for src, src_pot, c in ((own_ref, ownp_ref, core), (oth_ref, othp_ref, 1 - core)):
        for i in range(32):
            zb, q = i // 4, i % 4
            for j in range(4):
                xp = 8 * q + 4 * c + j
                fld[0, 3 + xp, 8 + 6 * zb : 14 + 6 * zb, :] = src.at[i][pl.ds(16 + j, 6, stride=4), :]
                pot[xp, 6 * zb : 6 * zb + 6, :] = src_pot.at[i][pl.ds(8 + j, 6, stride=4), :]

    half[:, pl.ds(pl.multiple_of(8 * core, 8), 8), :] = own_ref[:, 0:16, :].reshape(64, 8, 128)
    half[:, pl.ds(pl.multiple_of(8 - 8 * core, 8), 8), :] = oth_ref[:, 0:16, :].reshape(64, 8, 128)
    slot_lane = lax.broadcasted_iota(jnp.int32, (16, 128), 1) & 63
    in_slot = [(slot_lane >= 10 * n) & (slot_lane < 10 * n + 10) for n in range(6)]

    def expand(a, carry):
        xs = jnp.minimum(x_ref[a] >> 1, 26)
        y0 = y_ref[a]
        z0 = z_ref[a]
        begin = 4 * z0 - 6 * first_row(z0)
        box = half[a]
        moved = [
            pltpu.roll(jnp.where(in_slot[n], box, 0.0), (128 + y0 - 10 * n) & 127, 1) for n in range(6)
        ]
        high, rest = parts_of(jnp.concatenate(moved, axis=0))
        pick = pick_ref[4 * begin + (xs & 7)]
        got = jnp.dot(pick, high, preferred_element_type=F32)
        got = got + jnp.dot(pick, rest, preferred_element_type=F32)
        tiles[pl.ds(6 * a, 6)] = got.reshape(6, 16, 128)
        return carry

    lax.fori_loop(0, 64, expand, 0, unroll=16)

    ones = jnp.ones((128, 128), F32)
    low_half = lax.broadcasted_iota(jnp.int32, (8, 128), 1) < 64
    high_y = tapy_ref[:, 0:128]

    def step(cur, nxt, prev, ca, cb, cg):
        def inner(a, carry):
            xs = jnp.minimum(x_ref[a] >> 1, 26)
            z0 = z_ref[a]
            win = fld[cur, pl.ds(3 + xs, 6), pl.ds(8 + z0, 16), :]
            prod = jnp.sum(win * tiles[pl.ds(6 * a, 6)], axis=0)
            parts[pl.ds(a, 1), :] = jnp.sum(prod, axis=0, keepdims=True)
            return carry

        lax.fori_loop(0, 64, inner, 0, unroll=16)
        sums = jnp.dot(parts[...], ones, precision=HIGH, preferred_element_type=F32)
        scaled[...] = sums

        def along_yz(t, carry):
            rows = fld[cur, pl.ds(3 + 4 * t, 4), 8:56, :]
            high = rows.astype(jnp.bfloat16)
            rest = (rows - high.astype(F32)).astype(jnp.bfloat16)
            flat, flat_rest = high.reshape(192, 128), rest.reshape(192, 128)
            got = jnp.dot(flat, tapy_ref[...], preferred_element_type=F32)
            got = got[:, 0:128] + got[:, 128:256]
            got = got + jnp.dot(flat_rest, high_y, preferred_element_type=F32)
            wide = jnp.concatenate([high[n] for n in range(4)], axis=1)
            wide_rest = jnp.concatenate([rest[n] for n in range(4)], axis=1)
            by_z = jnp.dot(tapz_ref[...], wide, preferred_element_type=F32)
            by_z = by_z[0:48] + by_z[48:96]
            by_z = by_z + jnp.dot(tapz_ref[0:48, :], wide_rest, preferred_element_type=F32)
            for n in range(4):
                fld[nxt, 3 + 4 * t + n, 8:56, :] = got[48 * n : 48 * n + 48] + by_z[:, 128 * n : 128 * n + 128]
            return carry

        lax.fori_loop(0, 8, along_yz, 0, unroll=8)

        def along_x(zt, carry):
            rows = pl.ds(pl.multiple_of(8 + 8 * zt, 8), 8)
            own_rows = pl.ds(pl.multiple_of(8 * zt, 8), 8)
            zero = jnp.zeros((8, 128), F32)
            line = {x: zero for x in (-3, -2, -1, 32, 33, 34, 35)}
            for x in range(3):
                line[x] = fld[cur, 3 + x, rows, :]

            def odd(x):
                total = KIN[1] * (line[x] + line[x - 1]) + KIN[3] * (line[x + 1] + line[x - 2])
                total = total + KIN[5] * (line[x + 2] + line[x - 3])
                return pltpu.roll(total, 64, 1)

            here = odd(0)
            for x in range(32):
                if x + 3 < 32:
                    line[x + 3] = fld[cur, 6 + x, rows, :]
                after = odd(x + 1)
                total = fld[nxt, 3 + x, rows, :] + jnp.where(low_half, here, after)
                total = total + (3.0 * KIN[0] + pot[x, own_rows, :]) * line[x]
                for o in (1, 2, 3):
                    total = total + KIN[2 * o] * (line[x + o] + line[x - o])
                total = ca * total
                if cb != 0.0:
                    total = total + cb * line[x]
                if cg != 0.0:
                    total = total + cg * fld[prev, 3 + x, rows, :]
                fld[nxt, 3 + x, rows, :] = total
                here = after
            return carry

        lax.fori_loop(0, 6, along_x, 0, unroll=2)

        def outer(a, carry):
            xs = jnp.minimum(x_ref[a] >> 1, 26)
            z0 = z_ref[a]
            win = (nxt, pl.ds(3 + xs, 6), pl.ds(8 + z0, 16), slice(None))
            weight = scaled[pl.ds(a, 1), :] * (strength_ref[a] * (ca / PROJ_CELLS))
            fld[win] = fld[win] + weight[None] * tiles[pl.ds(6 * a, 6)]
            return carry

        lax.fori_loop(0, 64, outer, 0, unroll=4)

    def send(which, place):
        for i in range(32):
            zb, q = i // 4, i % 4
            for j in range(4):
                xp = 8 * q + 4 * core + j
                for kh in range(2):
                    z = 8 + 6 * zb + 3 * kh
                    to = ((2 * j + kh) * 32 + i) * 6 + place
                    out_ref[to : to + 3, :] = fld[which, 3 + xp, z : z + 3, :]

    step(0, 1, 2, 1.0 / HALF, -CENTER / HALF, 0.0)
    step(1, 2, 0, 2.0 / HALF, -2.0 * CENTER / HALF, -1.0)
    step(2, 0, 1, 2.0 / HALF, -2.0 * CENTER / HALF, -1.0)
    step(0, 1, 2, 2.0 / HALF, -2.0 * CENTER / HALF, -1.0)
    step(1, 2, 0, 1.0, 0.0, 0.0)
    send(1, 0)
    send(2, 3)


def band_matrix(n, blocks):
    taps = np.zeros((n * blocks, n * blocks), np.float32)
    for b in range(blocks):
        for k in range(n):
            for o in range(1, 7):
                for to in (k - o, k + o):
                    if 0 <= to < n:
                        taps[b * n + k, b * n + to] = KIN[o]
    return taps


def box_rows():
    pick = np.zeros((24, 96, 96), np.float32)
    for begin in (0, 2, 4):
        for first in range(8):
            for w in range(6):
                xp = first + w
                for z in range(10):
                    row, slot = divmod(begin + xp % 4 + 4 * z, 6)
                    pick[4 * begin + first, 16 * w + z, 16 * slot + 8 * (xp // 4 % 2) + row] = 1.0
    return pick


def two_parts(taps, axis):
    high = jnp.asarray(taps).astype(jnp.bfloat16)
    rest = (jnp.asarray(taps) - high.astype(F32)).astype(jnp.bfloat16)
    return jnp.concatenate([high, rest], axis=axis)


def same_core():
    return [[2 * i + c for i in range(32)] for c in range(2)]


def same_core_all():
    return [[(2 * i + c) * 8 + y for y in range(8) for i in range(32)] for c in range(2)]


def near_groups():
    return [
        [(16 * (2 * h + u) + 2 * x + c) * 8 + y for x in range(8) for u in range(2)]
        for h in range(2)
        for c in range(2)
        for y in range(8)
    ]


def far_groups():
    return [
        [(16 * (2 * h + u) + 2 * x + c) * 8 + y for h in range(2) for y in range(8)]
        for x in range(8)
        for c in range(2)
        for u in range(2)
    ]


def exchange(values, groups):
    return lax.all_to_all(values, ("dom", "band"), 0, 0, tiled=True, axis_index_groups=groups)


def pack(at, proj, pot):
    return pl.pallas_call(
        pack_kernel,
        out_shape=jax.ShapeDtypeStruct((32, P1_ROWS, 128), F32),
        in_specs=[smem()] * 3 + [vmem()] * 2,
        out_specs=vmem(),
        scratch_shapes=[pltpu.VMEM((64, 48, 128), F32)],
        compiler_params=params(56),
        name="pack",
    )(*at, proj, pot)


def boxes(at, got, orb):
    return pl.pallas_call(
        boxes_kernel,
        out_shape=jax.ShapeDtypeStruct((32, P2_ROWS, 128), F32),
        in_specs=[smem()] + [vmem()] * 2,
        out_specs=vmem(),
        scratch_shapes=[pltpu.VMEM((2, 40, 128), F32)],
        compiler_params=params(6),
        name="boxes",
    )(at[0], got, orb)


def chebyshev(at, strength, own, oth, own_pot, oth_pot):
    tapy = two_parts(band_matrix(NY, 2), 1)
    tapz = two_parts(band_matrix(48, 1), 0)
    return pl.pallas_call(
        filter_kernel,
        out_shape=jax.ShapeDtypeStruct((1536, 128), F32),
        in_specs=[smem()] * 4 + [vmem()] * 7,
        out_specs=vmem(),
        scratch_shapes=[
            pltpu.VMEM((3, 38, 64, 128), F32),
            pltpu.VMEM((32, 48, 128), F32),
            pltpu.VMEM((64, 16, 128), F32),
            pltpu.VMEM((64 * 6, 16, 128), F32),
            pltpu.VMEM((64, 128), F32),
            pltpu.VMEM((64, 128), F32),
        ],
        compiler_params=params(24),
        name="chebyshev",
    )(*at, strength, tapy, tapz, jnp.asarray(box_rows(), jnp.bfloat16), own, oth, own_pot, oth_pot)


def dot(a, b):
    return jnp.dot(a, b, precision=HIGH, preferred_element_type=F32)


def dot_t(a, b):
    return lax.dot_general(a, b, (((1,), (1,)), ((), ())), precision=HIGH, preferred_element_type=F32)


def parts_of(a):
    high = a.astype(jnp.bfloat16)
    return high, (a - high.astype(F32)).astype(jnp.bfloat16)


def dot_parts(a, b, turn=False):
    dims = (((1,), (1 if turn else 0,)), ((), ()))
    (ah, ar), (bh, br) = a, b
    total = lax.dot_general(ah, br, dims, preferred_element_type=F32)
    total = total + lax.dot_general(ar, bh, dims, preferred_element_type=F32)
    return total + lax.dot_general(ah, bh, dims, preferred_element_type=F32)


def gram_kernel(both_ref, mine_ref, other_ref, f_ref):
    core = place()[0] & 1
    f = [both_ref[pl.ds(r, 256, stride=6), :] for r in range(3)]
    for r in range(3):
        f_ref[r] = f[r]
    f = jnp.concatenate(f, axis=1)
    g = jnp.concatenate([both_ref[pl.ds(3 + r, 256, stride=6), :] for r in range(3)], axis=1)
    f = parts_of(f)
    corr = dot_parts(f, f, True)
    ham = dot_parts(f, parts_of(g), True)
    row = lax.broadcasted_iota(jnp.int32, (256, 256), 0)
    col = lax.broadcasted_iota(jnp.int32, (256, 256), 1)
    packed = jnp.where(row >= col, corr, ham)
    diag = jnp.sum(jnp.where(row == col, ham, 0.0), axis=0, keepdims=True)
    for ref, first in ((mine_ref, core == 0), (other_ref, core == 1)):
        half = jnp.where(first, packed[:, 0:128], packed[:, 128:256])
        for q in range(16):
            ref[q, 0:16, :] = half[16 * q : 16 * q + 16]
            ref[q, 16:24, :] = jnp.zeros((8, 128), F32)
        ref[0, 16:17, :] = jnp.where(first, diag[:, 0:128], diag[:, 128:256])


def ortho_kernel(own_ref, oth_ref, rows_ref, proj_ref, corr, ham, inv, work):
    me, block = place()
    core = me & 1
    row = lax.broadcasted_iota(jnp.int32, (256, 256), 0)
    col = lax.broadcasted_iota(jnp.int32, (256, 256), 1)
    below = row > col
    same = row == col
    scale = 1.0 / NCELLS
    diag = []
    for h in range(2):
        for q in range(16):
            half = jnp.where(core == h, own_ref[q, 0:16, :], oth_ref[q, 0:16, :])
            work[16 * q : 16 * q + 16, 128 * h : 128 * h + 128] = half
        diag.append(jnp.where(core == h, own_ref[0, 16:17, :], oth_ref[0, 16:17, :]))
    packed = work[...] * scale
    turned = packed.T
    diag = jnp.concatenate(diag, axis=1) * scale
    corr[...] = jnp.where(row >= col, packed, turned)
    ham[...] = jnp.where(same, diag, jnp.where(below, turned, packed))

    def half_lower(e):
        return jnp.where(below, e, jnp.where(same, 0.5 * e, 0.0))

    own = jnp.where(same, corr[...], 0.0)
    by_col = lax.rsqrt(jnp.sum(own, axis=0, keepdims=True))
    by_row = lax.rsqrt(jnp.sum(own, axis=1, keepdims=True))
    first = half_lower(by_row * corr[...] * by_col - jnp.where(same, 1.0, 0.0))
    inv[...] = jnp.where(same, by_col, 0.0) - first * by_col

    def rough(a, b, turn=False):
        dims = (((1,), (1 if turn else 0,)), ((), ()))
        return lax.dot_general(
            a.astype(jnp.bfloat16), b.astype(jnp.bfloat16), dims, preferred_element_type=F32
        )

    for _ in range(2):
        x = inv[...]
        e = rough(rough(x, corr[...]), x, True) - jnp.where(same, 1.0, 0.0)
        inv[...] = x - rough(half_lower(e), x)

    def refine(state):
        count, _ = state
        x = inv[...]
        e = dot_t(dot(x, corr[...]), x) - jnp.where(same, 1.0, 0.0)
        inv[...] = x - dot(half_lower(e), x)
        return count + 1, jnp.sum(e * e)

    def going(state):
        count, size = state
        return (count < 8) & jnp.logical_not(size < 1e-6)

    _, size = lax.while_loop(going, refine, (jnp.int32(0), jnp.float32(1.0)))
    least = jnp.min(jnp.where(same, inv[...], 1.0))

    @pl.when(jnp.logical_not((size < 1e-6) & (least > 0.0)))
    def _():
        work[...] = corr[...]
        inv[...] = jnp.where(same, 1.0, 0.0)

        def column(j, carry):
            picked = jnp.sum(jnp.where(col == j, work[...], 0.0), axis=1, keepdims=True)
            at_j = lax.broadcasted_iota(jnp.int32, (256, 1), 0)
            pivot = jnp.sum(jnp.where(at_j == j, picked, 0.0), axis=0, keepdims=True)
            factor = 1.0 / jnp.sqrt(pivot)
            inv[pl.ds(j, 1), :] = inv[pl.ds(j, 1), :] * factor
            down = jnp.where(at_j > j, picked, 0.0) * factor
            work[...] = work[...] - down * (work[pl.ds(j, 1), :] * factor)
            inv[...] = inv[...] - down * inv[pl.ds(j, 1), :]
            return carry

        lax.fori_loop(0, 256, column, 0)

    x = inv[...]
    mine = inv[pl.ds(pl.multiple_of(32 * block, 32), 32), :]
    proj_ref[...] = dot_t(dot(mine, ham[...]), x)
    rows_ref[...] = mine


def rotate_kernel(rows_ref, every_ref, out_ref):
    part = pl.program_id(0)
    first = 12 * (part & 1) + (part >> 1)
    f = jnp.concatenate([every_ref[t] for t in range(3)], axis=1)
    turned = dot_parts(parts_of(rows_ref[...]), parts_of(f))
    for t in range(3):
        out_ref[pl.ds(first + 4 * t, 32, stride=24), :] = turned[:, 128 * t : 128 * t + 128]


def gram(both):
    return pl.pallas_call(
        gram_kernel,
        out_shape=[jax.ShapeDtypeStruct((16, 24, 128), F32)] * 2 + [jax.ShapeDtypeStruct((3, 256, 128), F32)],
        in_specs=[vmem()],
        out_specs=[vmem()] * 3,
        compiler_params=params(8),
        name="gram",
    )(both)


def ortho(own, oth):
    return pl.pallas_call(
        ortho_kernel,
        out_shape=[jax.ShapeDtypeStruct((32, 256), F32)] * 2,
        in_specs=[vmem()] * 2,
        out_specs=[vmem()] * 2,
        scratch_shapes=[pltpu.VMEM((256, 256), F32)] * 4,
        compiler_params=params(8),
        name="ortho",
    )(own, oth)


def rotate(rows, every):
    return pl.pallas_call(
        rotate_kernel,
        out_shape=jax.ShapeDtypeStruct((768, 128), F32),
        grid=(8,),
        in_specs=[
            pl.BlockSpec((32, 256), lambda part: (0, 0)),
            pl.BlockSpec((3, 256, 128), lambda part: (part, 0, 0)),
        ],
        out_specs=pl.BlockSpec((768, 128), lambda part: (0, 0)),
        compiler_params=params(56),
        name="rotate",
    )(rows, every)


def swap_cores(values):
    return lax.ppermute(values, "dom", [(i, i ^ 1) for i in range(64)])


def sum_everywhere(values):
    for groups in (near_groups(), far_groups()):
        part = jnp.sum(exchange(values, groups), axis=0)
        values = jnp.broadcast_to(part[None], values.shape)
    return exchange(values, near_groups())


def on_device(orbitals, potential, proj_shape, proj_strength, atom_z, atom_x, atom_y):
    at = (atom_z, atom_x, atom_y)
    first = pack(at, proj_shape.reshape(64, 24, 128), potential.reshape(24, 128))
    first = lax.all_to_all(first, "dom", 0, 0, tiled=True, axis_index_groups=same_core())
    first_oth = swap_cores(first)
    second = boxes(at, first, orbitals.reshape(32, 24, 128))
    second, first_oth = lax.optimization_barrier((second, first_oth))
    second = lax.all_to_all(second, "dom", 0, 0, tiled=True, axis_index_groups=same_core())
    second_oth = swap_cores(second)
    both = chebyshev(at, proj_strength, second, second_oth, first, first_oth)
    both = both.reshape(256, 3, 2, 128)
    both = exchange(both, same_core_all())
    both = both.reshape(1536, 128)
    mine, other, filtered = gram(both)
    every = lax.all_gather(filtered, "band", axis=0, tiled=True)
    mine = sum_everywhere(mine + swap_cores(other))
    rows, projected = ortho(mine, swap_cores(mine))
    rotated = rotate(rows, every)
    return (rotated.reshape(32, 1, 6, 512), projected)


def solution(mesh):
    return jax.shard_map(
        on_device,
        mesh=mesh,
        in_specs=(
            P("band", "dom", None, None),
            P("dom", None, None),
            P(None, "dom", None, None),
            P(),
            P(),
            P(),
            P(),
        ),
        out_specs=(P("band", "dom", None, None), P("band", None)),
        check_vma=False,
    )
```

```python
import jax
import jax.numpy as jnp
import numpy as np
from jax import lax
from jax.experimental import pallas as pl
from jax.experimental.pallas import tpu as pltpu
from jax.sharding import PartitionSpec as P

NY = 64
NCELLS = 196608
PROJ_CELLS = 1000
COEFFS = [
    -5369.0 / 1800.0,
    12.0 / 7.0,
    -15.0 / 56.0,
    10.0 / 189.0,
    -1.0 / 112.0,
    2.0 / 1925.0,
    -1.0 / 16632.0,
]
CENTER = 9.5
HALF = 6.5
KIN = [-0.5 * c for c in COEFFS]
HIGH = lax.Precision.HIGHEST
F32 = jnp.float32


P1_ROWS = 32
P2_ROWS = 40


def place():
    return lax.axis_index("dom"), lax.axis_index("band")


def vmem():
    return pl.BlockSpec(memory_space=pltpu.VMEM)


def smem():
    return pl.BlockSpec(memory_space=pltpu.SMEM)


def params(megabytes):
    return pltpu.CompilerParams(vmem_limit_bytes=megabytes * 1024 * 1024)


def pack_kernel(z_ref, x_ref, y_ref, proj_ref, pot_ref, out_ref, pad_ref):
    me, _ = place()
    z_first = (me >> 3) * 6
    x_first = (me & 7) * 8
    pad_ref[:, 24:48, :] = jnp.zeros((64, 24, 128), F32)
    pad_ref[:, 0:24, :] = proj_ref[...]
    lane = lax.broadcasted_iota(jnp.int32, (8, 128), 1)
    sub = lax.broadcasted_iota(jnp.int32, (8, 128), 0)
    slot_lane = lane % 64
    z_cells, x_cells, slots = [], [], []
    for s in range(6):
        row = s + 6 * sub
        z_cells.append(z_first + row // 4)
        x_cells.append(x_first + 2 * (row % 4) + lane // 64)
        slots.append((slot_lane >= 10 * s) & (slot_lane < 10 * s + 10))

    def pair(i, carry):
        for m in range(2):
            a = 2 * i + m
            z0 = z_ref[a]
            x0 = x_ref[a]
            y0 = y_ref[a]
            packed = jnp.zeros((8, 128), F32)
            for s in range(6):
                z, x = z_cells[s], x_cells[s]
                inside = (z >= z0) & (z < z0 + 10) & (x >= x0) & (x < x0 + 10)
                rows = pad_ref[a, pl.ds(s, 8, stride=6), :]
                rows = jnp.where(inside, rows, 0.0)
                rows = pltpu.roll(rows, (128 + 10 * s - y0) & 127, 1)
                packed = jnp.where(slots[s], rows, packed)
            out_ref[i, pl.ds(4 * m, 4), :] = packed[0:4]
        out_ref[i, pl.ds(8, 24), :] = pot_ref[...]
        return carry

    lax.fori_loop(0, 32, pair, 0, unroll=4)


def first_row(z0):
    return (4 * z0 * 171) >> 10


def boxes_kernel(z_ref, got_ref, orb_ref, out_ref, col_ref):
    me, _ = place()
    col_ref[...] = jnp.zeros_like(col_ref)
    for zb in range(8):
        part = got_ref[4 * zb, 0:8, :]
        for q in range(1, 4):
            part = part + got_ref[4 * zb + q, 0:8, :]
        col_ref[0, 4 * zb : 4 * zb + 4, :] = part[0:4]
        col_ref[1, 4 * zb : 4 * zb + 4, :] = part[4:8]
    boxes = []
    for m in range(2):
        z0 = z_ref[2 * (me >> 1) + m]
        boxes.append(col_ref[m, pl.ds(first_row(z0), 8), :])

    def send(n, carry):
        out_ref[n, 0:8, :] = boxes[0]
        out_ref[n, 8:16, :] = boxes[1]
        out_ref[n, 16:40, :] = orb_ref[n]
        return carry

    lax.fori_loop(0, 32, send, 0, unroll=4)


def filter_kernel(
    z_ref, x_ref, y_ref, strength_ref, tapy_ref, tapz_ref, pick_ref, own_ref, oth_ref, ownp_ref, othp_ref, out_ref,
    fld, pot, half, tiles, parts, scaled,
):
    core = place()[0] & 1
    for edge in (slice(0, 3), slice(35, 38)):
        fld[:, edge, :, :] = jnp.zeros((3, 3, 64, 128), F32)
    for edge in (slice(0, 8), slice(56, 64)):
        fld[:, 3:35, edge, :] = jnp.zeros((3, 32, 8, 128), F32)
    for src, src_pot, c in ((own_ref, ownp_ref, core), (oth_ref, othp_ref, 1 - core)):
        for i in range(32):
            zb, q = i // 4, i % 4
            for j in range(4):
                xp = 8 * q + 4 * c + j
                fld[0, 3 + xp, 8 + 6 * zb : 14 + 6 * zb, :] = src.at[i][pl.ds(16 + j, 6, stride=4), :]
                pot[xp, 6 * zb : 6 * zb + 6, :] = src_pot.at[i][pl.ds(8 + j, 6, stride=4), :]

    half[:, pl.ds(pl.multiple_of(8 * core, 8), 8), :] = own_ref[:, 0:16, :].reshape(64, 8, 128)
    half[:, pl.ds(pl.multiple_of(8 - 8 * core, 8), 8), :] = oth_ref[:, 0:16, :].reshape(64, 8, 128)
    slot_lane = lax.broadcasted_iota(jnp.int32, (16, 128), 1) & 63
    in_slot = [(slot_lane >= 10 * n) & (slot_lane < 10 * n + 10) for n in range(6)]

    def expand(a, carry):
        xs = jnp.minimum(x_ref[a] >> 1, 26)
        y0 = y_ref[a]
        z0 = z_ref[a]
        begin = 4 * z0 - 6 * first_row(z0)
        box = half[a]
        moved = [
            pltpu.roll(jnp.where(in_slot[n], box, 0.0), (128 + y0 - 10 * n) & 127, 1) for n in range(6)
        ]
        high, rest = parts_of(jnp.concatenate(moved, axis=0))
        pick = pick_ref[4 * begin + (xs & 7)]
        got = jnp.dot(pick, high, preferred_element_type=F32)
        got = got + jnp.dot(pick, rest, preferred_element_type=F32)
        tiles[pl.ds(6 * a, 6)] = got.reshape(6, 16, 128)
        return carry

    lax.fori_loop(0, 64, expand, 0, unroll=16)

    ones = jnp.ones((128, 128), F32)
    low_half = lax.broadcasted_iota(jnp.int32, (8, 128), 1) < 64
    high_y = tapy_ref[:, 0:128]

    def step(cur, nxt, prev, ca, cb, cg):
        def inner(a, carry):
            xs = jnp.minimum(x_ref[a] >> 1, 26)
            z0 = z_ref[a]
            win = fld[cur, pl.ds(3 + xs, 6), pl.ds(8 + z0, 16), :]
            prod = jnp.sum(win * tiles[pl.ds(6 * a, 6)], axis=0)
            parts[pl.ds(a, 1), :] = jnp.sum(prod, axis=0, keepdims=True)
            return carry

        lax.fori_loop(0, 64, inner, 0, unroll=16)
        sums = jnp.dot(parts[...], ones, precision=HIGH, preferred_element_type=F32)
        scaled[...] = sums

        def along_yz(t, carry):
            rows = fld[cur, pl.ds(3 + 4 * t, 4), 8:56, :]
            high = rows.astype(jnp.bfloat16)
            rest = (rows - high.astype(F32)).astype(jnp.bfloat16)
            flat, flat_rest = high.reshape(192, 128), rest.reshape(192, 128)
            got = jnp.dot(flat, tapy_ref[...], preferred_element_type=F32)
            got = got[:, 0:128] + got[:, 128:256]
            got = got + jnp.dot(flat_rest, high_y, preferred_element_type=F32)
            wide = jnp.concatenate([high[n] for n in range(4)], axis=1)
            wide_rest = jnp.concatenate([rest[n] for n in range(4)], axis=1)
            by_z = jnp.dot(tapz_ref[...], wide, preferred_element_type=F32)
            by_z = by_z[0:48] + by_z[48:96]
            by_z = by_z + jnp.dot(tapz_ref[0:48, :], wide_rest, preferred_element_type=F32)
            for n in range(4):
                fld[nxt, 3 + 4 * t + n, 8:56, :] = got[48 * n : 48 * n + 48] + by_z[:, 128 * n : 128 * n + 128]
            return carry

        lax.fori_loop(0, 8, along_yz, 0, unroll=8)

        def along_x(zt, carry):
            rows = pl.ds(pl.multiple_of(8 + 8 * zt, 8), 8)
            own_rows = pl.ds(pl.multiple_of(8 * zt, 8), 8)
            zero = jnp.zeros((8, 128), F32)
            line = {x: zero for x in (-3, -2, -1, 32, 33, 34, 35)}
            for x in range(3):
                line[x] = fld[cur, 3 + x, rows, :]

            def odd(x):
                total = KIN[1] * (line[x] + line[x - 1]) + KIN[3] * (line[x + 1] + line[x - 2])
                total = total + KIN[5] * (line[x + 2] + line[x - 3])
                return pltpu.roll(total, 64, 1)

            here = odd(0)
            for x in range(32):
                if x + 3 < 32:
                    line[x + 3] = fld[cur, 6 + x, rows, :]
                after = odd(x + 1)
                total = fld[nxt, 3 + x, rows, :] + jnp.where(low_half, here, after)
                total = total + (3.0 * KIN[0] + pot[x, own_rows, :]) * line[x]
                for o in (1, 2, 3):
                    total = total + KIN[2 * o] * (line[x + o] + line[x - o])
                total = ca * total
                if cb != 0.0:
                    total = total + cb * line[x]
                if cg != 0.0:
                    total = total + cg * fld[prev, 3 + x, rows, :]
                fld[nxt, 3 + x, rows, :] = total
                here = after
            return carry

        lax.fori_loop(0, 6, along_x, 0, unroll=2)

        def outer(a, carry):
            xs = jnp.minimum(x_ref[a] >> 1, 26)
            z0 = z_ref[a]
            win = (nxt, pl.ds(3 + xs, 6), pl.ds(8 + z0, 16), slice(None))
            weight = scaled[pl.ds(a, 1), :] * (strength_ref[a] * (ca / PROJ_CELLS))
            fld[win] = fld[win] + weight[None] * tiles[pl.ds(6 * a, 6)]
            return carry

        lax.fori_loop(0, 64, outer, 0, unroll=4)

    def send(which, place):
        for i in range(32):
            zb, q = i // 4, i % 4
            for j in range(4):
                xp = 8 * q + 4 * core + j
                for kh in range(2):
                    z = 8 + 6 * zb + 3 * kh
                    to = ((2 * j + kh) * 32 + i) * 6 + place
                    out_ref[to : to + 3, :] = fld[which, 3 + xp, z : z + 3, :]

    step(0, 1, 2, 1.0 / HALF, -CENTER / HALF, 0.0)
    step(1, 2, 0, 2.0 / HALF, -2.0 * CENTER / HALF, -1.0)
    step(2, 0, 1, 2.0 / HALF, -2.0 * CENTER / HALF, -1.0)
    step(0, 1, 2, 2.0 / HALF, -2.0 * CENTER / HALF, -1.0)
    step(1, 2, 0, 1.0, 0.0, 0.0)
    send(1, 0)
    send(2, 3)


def band_matrix(n, blocks):
    taps = np.zeros((n * blocks, n * blocks), np.float32)
    for b in range(blocks):
        for k in range(n):
            for o in range(1, 7):
                for to in (k - o, k + o):
                    if 0 <= to < n:
                        taps[b * n + k, b * n + to] = KIN[o]
    return taps


def box_rows():
    pick = np.zeros((24, 96, 96), np.float32)
    for begin in (0, 2, 4):
        for first in range(8):
            for w in range(6):
                xp = first + w
                for z in range(10):
                    row, slot = divmod(begin + xp % 4 + 4 * z, 6)
                    pick[4 * begin + first, 16 * w + z, 16 * slot + 8 * (xp // 4 % 2) + row] = 1.0
    return pick


def two_parts(taps, axis):
    high = jnp.asarray(taps).astype(jnp.bfloat16)
    rest = (jnp.asarray(taps) - high.astype(F32)).astype(jnp.bfloat16)
    return jnp.concatenate([high, rest], axis=axis)


def same_core():
    return [[2 * i + c for i in range(32)] for c in range(2)]


def same_core_all():
    return [[(2 * i + c) * 8 + y for y in range(8) for i in range(32)] for c in range(2)]


def near_groups():
    return [
        [(16 * z + 2 * x + c) * 8 + 2 * t + u for x in range(8) for u in range(2)]
        for z in range(4)
        for c in range(2)
        for t in range(4)
    ]


def far_groups():
    return [
        [(16 * z + 2 * x + c) * 8 + 2 * t + u for z in range(4) for t in range(4)]
        for x in range(8)
        for c in range(2)
        for u in range(2)
    ]


def exchange(values, groups):
    return lax.all_to_all(values, ("dom", "band"), 0, 0, tiled=True, axis_index_groups=groups)


def pack(at, proj, pot):
    return pl.pallas_call(
        pack_kernel,
        out_shape=jax.ShapeDtypeStruct((32, P1_ROWS, 128), F32),
        in_specs=[smem()] * 3 + [vmem()] * 2,
        out_specs=vmem(),
        scratch_shapes=[pltpu.VMEM((64, 48, 128), F32)],
        compiler_params=params(56),
        name="pack",
    )(*at, proj, pot)


def boxes(at, got, orb):
    return pl.pallas_call(
        boxes_kernel,
        out_shape=jax.ShapeDtypeStruct((32, P2_ROWS, 128), F32),
        in_specs=[smem()] + [vmem()] * 2,
        out_specs=vmem(),
        scratch_shapes=[pltpu.VMEM((2, 40, 128), F32)],
        compiler_params=params(56),
        name="boxes",
    )(at[0], got, orb)


def chebyshev(at, strength, own, oth, own_pot, oth_pot):
    tapy = two_parts(band_matrix(NY, 2), 1)
    tapz = two_parts(band_matrix(48, 1), 0)
    return pl.pallas_call(
        filter_kernel,
        out_shape=jax.ShapeDtypeStruct((1536, 128), F32),
        in_specs=[smem()] * 4 + [vmem()] * 7,
        out_specs=vmem(),
        scratch_shapes=[
            pltpu.VMEM((3, 38, 64, 128), F32),
            pltpu.VMEM((32, 48, 128), F32),
            pltpu.VMEM((64, 16, 128), F32),
            pltpu.VMEM((64 * 6, 16, 128), F32),
            pltpu.VMEM((64, 128), F32),
            pltpu.VMEM((64, 128), F32),
        ],
        compiler_params=params(24),
        name="chebyshev",
    )(*at, strength, tapy, tapz, jnp.asarray(box_rows(), jnp.bfloat16), own, oth, own_pot, oth_pot)


def dot(a, b):
    return jnp.dot(a, b, precision=HIGH, preferred_element_type=F32)


def dot_t(a, b):
    return lax.dot_general(a, b, (((1,), (1,)), ((), ())), precision=HIGH, preferred_element_type=F32)


def parts_of(a):
    high = a.astype(jnp.bfloat16)
    return high, (a - high.astype(F32)).astype(jnp.bfloat16)


def dot_parts(a, b, turn=False):
    dims = (((1,), (1 if turn else 0,)), ((), ()))
    (ah, ar), (bh, br) = a, b
    total = lax.dot_general(ah, br, dims, preferred_element_type=F32)
    total = total + lax.dot_general(ar, bh, dims, preferred_element_type=F32)
    return total + lax.dot_general(ah, bh, dims, preferred_element_type=F32)


def gram_kernel(both_ref, mine_ref, other_ref, f_ref):
    core = place()[0] & 1
    f = [both_ref[pl.ds(r, 256, stride=6), :] for r in range(3)]
    for r in range(3):
        f_ref[r] = f[r]
    f = jnp.concatenate(f, axis=1)
    g = jnp.concatenate([both_ref[pl.ds(3 + r, 256, stride=6), :] for r in range(3)], axis=1)
    f = parts_of(f)
    corr = dot_parts(f, f, True)
    ham = dot_parts(f, parts_of(g), True)
    row = lax.broadcasted_iota(jnp.int32, (256, 256), 0)
    col = lax.broadcasted_iota(jnp.int32, (256, 256), 1)
    packed = jnp.where(row >= col, corr, ham)
    diag = jnp.sum(jnp.where(row == col, ham, 0.0), axis=0, keepdims=True)
    for ref, first in ((mine_ref, core == 0), (other_ref, core == 1)):
        half = jnp.where(first, packed[:, 0:128], packed[:, 128:256])
        for q in range(16):
            ref[q, 0:16, :] = half[16 * q : 16 * q + 16]
            ref[q, 16:24, :] = jnp.zeros((8, 128), F32)
        ref[0, 16:17, :] = jnp.where(first, diag[:, 0:128], diag[:, 128:256])


def ortho_kernel(own_ref, oth_ref, every_ref, rot_ref, proj_ref, corr, ham, inv, work, every, arrived):
    fetch = pltpu.make_async_copy(every_ref, every, arrived)
    fetch.start()
    me, block = place()
    core = me & 1
    row = lax.broadcasted_iota(jnp.int32, (256, 256), 0)
    col = lax.broadcasted_iota(jnp.int32, (256, 256), 1)
    below = row > col
    same = row == col
    scale = 1.0 / NCELLS
    diag = []
    for h in range(2):
        for q in range(16):
            half = jnp.where(core == h, own_ref[q, 0:16, :], oth_ref[q, 0:16, :])
            work[16 * q : 16 * q + 16, 128 * h : 128 * h + 128] = half
        diag.append(jnp.where(core == h, own_ref[0, 16:17, :], oth_ref[0, 16:17, :]))
    packed = work[...] * scale
    turned = packed.T
    diag = jnp.concatenate(diag, axis=1) * scale
    corr[...] = jnp.where(row >= col, packed, turned)
    ham[...] = jnp.where(same, diag, jnp.where(below, turned, packed))

    def half_lower(e):
        return jnp.where(below, e, jnp.where(same, 0.5 * e, 0.0))

    own = jnp.where(same, corr[...], 0.0)
    by_col = lax.rsqrt(jnp.sum(own, axis=0, keepdims=True))
    by_row = lax.rsqrt(jnp.sum(own, axis=1, keepdims=True))
    first = half_lower(by_row * corr[...] * by_col - jnp.where(same, 1.0, 0.0))
    inv[...] = jnp.where(same, by_col, 0.0) - first * by_col

    def rough(a, b, turn=False):
        dims = (((1,), (1 if turn else 0,)), ((), ()))
        return lax.dot_general(
            a.astype(jnp.bfloat16), b.astype(jnp.bfloat16), dims, preferred_element_type=F32
        )

    for _ in range(2):
        x = inv[...]
        e = rough(rough(x, corr[...]), x, True) - jnp.where(same, 1.0, 0.0)
        inv[...] = x - rough(half_lower(e), x)

    def refine(state):
        count, _ = state
        x = inv[...]
        e = dot_t(dot(x, corr[...]), x) - jnp.where(same, 1.0, 0.0)
        inv[...] = x - dot(half_lower(e), x)
        return count + 1, jnp.sum(e * e)

    def going(state):
        count, size = state
        return (count < 8) & jnp.logical_not(size < 1e-6)

    _, size = lax.while_loop(going, refine, (jnp.int32(0), jnp.float32(1.0)))
    least = jnp.min(jnp.where(same, inv[...], 1.0))

    @pl.when(jnp.logical_not((size < 1e-6) & (least > 0.0)))
    def _():
        work[...] = corr[...]
        inv[...] = jnp.where(same, 1.0, 0.0)

        def column(j, carry):
            picked = jnp.sum(jnp.where(col == j, work[...], 0.0), axis=1, keepdims=True)
            at_j = lax.broadcasted_iota(jnp.int32, (256, 1), 0)
            pivot = jnp.sum(jnp.where(at_j == j, picked, 0.0), axis=0, keepdims=True)
            factor = 1.0 / jnp.sqrt(pivot)
            inv[pl.ds(j, 1), :] = inv[pl.ds(j, 1), :] * factor
            down = jnp.where(at_j > j, picked, 0.0) * factor
            work[...] = work[...] - down * (work[pl.ds(j, 1), :] * factor)
            inv[...] = inv[...] - down * inv[pl.ds(j, 1), :]
            return carry

        lax.fori_loop(0, 256, column, 0)

    x = inv[...]
    mine = inv[pl.ds(pl.multiple_of(32 * block, 32), 32), :]
    proj_ref[...] = dot_t(dot(mine, ham[...]), x)
    rows = parts_of(mine)
    fetch.wait()
    for part in range(8):
        j, kh = part // 2, part % 2
        f = jnp.concatenate([every[3 * part + t] for t in range(3)], axis=1)
        turned = dot_parts(rows, parts_of(f))
        for t in range(3):
            rot_ref[pl.ds((3 * kh + t) * 4 + j, 32, stride=24), :] = turned[:, 128 * t : 128 * t + 128]


def gram(both):
    return pl.pallas_call(
        gram_kernel,
        out_shape=[jax.ShapeDtypeStruct((16, 24, 128), F32)] * 2 + [jax.ShapeDtypeStruct((3, 256, 128), F32)],
        in_specs=[vmem()],
        out_specs=[vmem()] * 3,
        compiler_params=params(8),
        name="gram",
    )(both)


def ortho(own, oth, every):
    return pl.pallas_call(
        ortho_kernel,
        out_shape=[jax.ShapeDtypeStruct((768, 128), F32), jax.ShapeDtypeStruct((32, 256), F32)],
        in_specs=[vmem(), vmem(), pl.BlockSpec(memory_space=pl.ANY)],
        out_specs=[vmem()] * 2,
        scratch_shapes=[pltpu.VMEM((256, 256), F32)] * 4
        + [pltpu.VMEM((24, 256, 128), F32), pltpu.SemaphoreType.DMA(())],
        compiler_params=params(56),
        name="ortho",
    )(own, oth, every)


def swap_cores(values):
    return lax.ppermute(values, "dom", [(i, i ^ 1) for i in range(64)])


def sum_everywhere(values):
    for groups in (near_groups(), far_groups()):
        part = jnp.sum(exchange(values, groups), axis=0)
        values = jnp.broadcast_to(part[None], values.shape)
    return exchange(values, near_groups())


def on_device(orbitals, potential, proj_shape, proj_strength, atom_z, atom_x, atom_y):
    at = (atom_z, atom_x, atom_y)
    first = pack(at, proj_shape.reshape(64, 24, 128), potential.reshape(24, 128))
    first = lax.all_to_all(first, "dom", 0, 0, tiled=True, axis_index_groups=same_core())
    first_oth = swap_cores(first)
    second = boxes(at, first, orbitals.reshape(32, 24, 128))
    second = lax.all_to_all(second, "dom", 0, 0, tiled=True, axis_index_groups=same_core())
    second_oth = swap_cores(second)
    both = chebyshev(at, proj_strength, second, second_oth, first, first_oth)
    both = both.reshape(256, 3, 2, 128)
    both = exchange(both, same_core_all())
    both = both.reshape(1536, 128)
    mine, other, filtered = gram(both)
    every = lax.all_gather(filtered, "band", axis=0, tiled=True)
    mine = sum_everywhere(mine + swap_cores(other))
    rotated, projected = ortho(mine, swap_cores(mine), every)
    return (rotated.reshape(32, 1, 6, 512), projected)


def solution(mesh):
    return jax.shard_map(
        on_device,
        mesh=mesh,
        in_specs=(
            P("band", "dom", None, None),
            P("dom", None, None),
            P(None, "dom", None, None),
            P(),
            P(),
            P(),
            P(),
        ),
        out_specs=(P("band", "dom", None, None), P("band", None)),
        check_vma=False,
    )
```

```python
import jax
import jax.numpy as jnp
import numpy as np
from jax import lax
from jax.experimental import pallas as pl
from jax.experimental.pallas import tpu as pltpu
from jax.sharding import PartitionSpec as P

NY = 64
NCELLS = 196608
PROJ_CELLS = 1000
COEFFS = [
    -5369.0 / 1800.0,
    12.0 / 7.0,
    -15.0 / 56.0,
    10.0 / 189.0,
    -1.0 / 112.0,
    2.0 / 1925.0,
    -1.0 / 16632.0,
]
CENTER = 9.5
HALF = 6.5
KIN = [-0.5 * c for c in COEFFS]
HIGH = lax.Precision.HIGHEST
F32 = jnp.float32


P1_ROWS = 32
P2_ROWS = 40


def place():
    return lax.axis_index("dom"), lax.axis_index("band")


def vmem():
    return pl.BlockSpec(memory_space=pltpu.VMEM)


def smem():
    return pl.BlockSpec(memory_space=pltpu.SMEM)


def params(megabytes):
    return pltpu.CompilerParams(vmem_limit_bytes=megabytes * 1024 * 1024)


def pack_kernel(z_ref, x_ref, y_ref, proj_ref, pot_ref, out_ref, pad_ref):
    me, _ = place()
    z_first = (me >> 3) * 6
    x_first = (me & 7) * 8
    pad_ref[:, 24:48, :] = jnp.zeros((64, 24, 128), F32)
    pad_ref[:, 0:24, :] = proj_ref[...]
    lane = lax.broadcasted_iota(jnp.int32, (8, 128), 1)
    sub = lax.broadcasted_iota(jnp.int32, (8, 128), 0)
    slot_lane = lane % 64
    z_cells, x_cells, slots = [], [], []
    for s in range(6):
        row = s + 6 * sub
        z_cells.append(z_first + row // 4)
        x_cells.append(x_first + 2 * (row % 4) + lane // 64)
        slots.append((slot_lane >= 10 * s) & (slot_lane < 10 * s + 10))

    def pair(i, carry):
        for m in range(2):
            a = 2 * i + m
            z0 = z_ref[a]
            x0 = x_ref[a]
            y0 = y_ref[a]
            packed = jnp.zeros((8, 128), F32)
            for s in range(6):
                z, x = z_cells[s], x_cells[s]
                inside = (z >= z0) & (z < z0 + 10) & (x >= x0) & (x < x0 + 10)
                rows = pad_ref[a, pl.ds(s, 8, stride=6), :]
                rows = jnp.where(inside, rows, 0.0)
                rows = pltpu.roll(rows, (128 + 10 * s - y0) & 127, 1)
                packed = jnp.where(slots[s], rows, packed)
            out_ref[i, pl.ds(4 * m, 4), :] = packed[0:4]
        out_ref[i, pl.ds(8, 24), :] = pot_ref[...]
        return carry

    lax.fori_loop(0, 32, pair, 0, unroll=4)


def first_row(z0):
    return (4 * z0 * 171) >> 10


def boxes_kernel(z_ref, got_ref, orb_ref, out_ref, col_ref):
    me, _ = place()
    col_ref[...] = jnp.zeros_like(col_ref)
    for zb in range(8):
        part = got_ref[4 * zb, 0:8, :]
        for q in range(1, 4):
            part = part + got_ref[4 * zb + q, 0:8, :]
        col_ref[0, 4 * zb : 4 * zb + 4, :] = part[0:4]
        col_ref[1, 4 * zb : 4 * zb + 4, :] = part[4:8]
    boxes = []
    for m in range(2):
        z0 = z_ref[2 * (me >> 1) + m]
        boxes.append(col_ref[m, pl.ds(first_row(z0), 8), :])

    def send(n, carry):
        out_ref[n, 0:8, :] = boxes[0]
        out_ref[n, 8:16, :] = boxes[1]
        out_ref[n, 16:40, :] = orb_ref[n]
        return carry

    lax.fori_loop(0, 32, send, 0, unroll=4)


def filter_kernel(
    z_ref, x_ref, y_ref, strength_ref, tapy_ref, tapz_ref, pick_ref, own_ref, oth_ref, ownp_ref, othp_ref, out_ref,
    fld, pot, half, tiles, parts, scaled,
):
    core = place()[0] & 1
    for edge in (slice(0, 3), slice(35, 38)):
        fld[:, edge, :, :] = jnp.zeros((3, 3, 64, 128), F32)
    for edge in (slice(0, 8), slice(56, 64)):
        fld[:, 3:35, edge, :] = jnp.zeros((3, 32, 8, 128), F32)
    for src, src_pot, c in ((own_ref, ownp_ref, core), (oth_ref, othp_ref, 1 - core)):
        for i in range(32):
            zb, q = i // 4, i % 4
            for j in range(4):
                xp = 8 * q + 4 * c + j
                fld[0, 3 + xp, 8 + 6 * zb : 14 + 6 * zb, :] = src.at[i][pl.ds(16 + j, 6, stride=4), :]
                pot[xp, 6 * zb : 6 * zb + 6, :] = src_pot.at[i][pl.ds(8 + j, 6, stride=4), :]

    half[:, pl.ds(pl.multiple_of(8 * core, 8), 8), :] = own_ref[:, 0:16, :].reshape(64, 8, 128)
    half[:, pl.ds(pl.multiple_of(8 - 8 * core, 8), 8), :] = oth_ref[:, 0:16, :].reshape(64, 8, 128)
    slot_lane = lax.broadcasted_iota(jnp.int32, (16, 128), 1) & 63
    in_slot = [(slot_lane >= 10 * n) & (slot_lane < 10 * n + 10) for n in range(6)]

    def expand(a, carry):
        xs = jnp.minimum(x_ref[a] >> 1, 26)
        y0 = y_ref[a]
        z0 = z_ref[a]
        begin = 4 * z0 - 6 * first_row(z0)
        box = half[a]
        moved = [
            pltpu.roll(jnp.where(in_slot[n], box, 0.0), (128 + y0 - 10 * n) & 127, 1) for n in range(6)
        ]
        high, rest = parts_of(jnp.concatenate(moved, axis=0))
        pick = pick_ref[4 * begin + (xs & 7)]
        got = jnp.dot(pick, high, preferred_element_type=F32)
        got = got + jnp.dot(pick, rest, preferred_element_type=F32)
        tiles[pl.ds(6 * a, 6)] = got.reshape(6, 16, 128)
        return carry

    lax.fori_loop(0, 64, expand, 0, unroll=16)

    ones = jnp.ones((128, 128), F32)
    low_half = lax.broadcasted_iota(jnp.int32, (8, 128), 1) < 64
    high_y = tapy_ref[:, 0:128]

    def step(cur, nxt, prev, ca, cb, cg):
        def inner(a, carry):
            xs = jnp.minimum(x_ref[a] >> 1, 26)
            z0 = z_ref[a]
            win = fld[cur, pl.ds(3 + xs, 6), pl.ds(8 + z0, 16), :]
            prod = jnp.sum(win * tiles[pl.ds(6 * a, 6)], axis=0)
            parts[pl.ds(a, 1), :] = jnp.sum(prod, axis=0, keepdims=True)
            return carry

        lax.fori_loop(0, 64, inner, 0, unroll=16)
        sums = jnp.dot(parts[...], ones, precision=HIGH, preferred_element_type=F32)
        scaled[...] = sums

        def along_yz(t, carry):
            rows = fld[cur, pl.ds(3 + 4 * t, 4), 8:56, :]
            high = rows.astype(jnp.bfloat16)
            rest = (rows - high.astype(F32)).astype(jnp.bfloat16)
            flat, flat_rest = high.reshape(192, 128), rest.reshape(192, 128)
            got = jnp.dot(flat, tapy_ref[...], preferred_element_type=F32)
            got = got[:, 0:128] + got[:, 128:256]
            got = got + jnp.dot(flat_rest, high_y, preferred_element_type=F32)
            wide = jnp.concatenate([high[n] for n in range(4)], axis=1)
            wide_rest = jnp.concatenate([rest[n] for n in range(4)], axis=1)
            by_z = jnp.dot(tapz_ref[...], wide, preferred_element_type=F32)
            by_z = by_z[0:48] + by_z[48:96]
            by_z = by_z + jnp.dot(tapz_ref[0:48, :], wide_rest, preferred_element_type=F32)
            for n in range(4):
                fld[nxt, 3 + 4 * t + n, 8:56, :] = got[48 * n : 48 * n + 48] + by_z[:, 128 * n : 128 * n + 128]
            return carry

        lax.fori_loop(0, 8, along_yz, 0, unroll=8)

        def along_x(zt, carry):
            rows = pl.ds(pl.multiple_of(8 + 8 * zt, 8), 8)
            own_rows = pl.ds(pl.multiple_of(8 * zt, 8), 8)
            zero = jnp.zeros((8, 128), F32)
            line = {x: zero for x in (-3, -2, -1, 32, 33, 34, 35)}
            for x in range(3):
                line[x] = fld[cur, 3 + x, rows, :]

            def odd(x):
                total = KIN[1] * (line[x] + line[x - 1]) + KIN[3] * (line[x + 1] + line[x - 2])
                total = total + KIN[5] * (line[x + 2] + line[x - 3])
                return pltpu.roll(total, 64, 1)

            here = odd(0)
            for x in range(32):
                if x + 3 < 32:
                    line[x + 3] = fld[cur, 6 + x, rows, :]
                after = odd(x + 1)
                total = fld[nxt, 3 + x, rows, :] + jnp.where(low_half, here, after)
                total = total + (3.0 * KIN[0] + pot[x, own_rows, :]) * line[x]
                for o in (1, 2, 3):
                    total = total + KIN[2 * o] * (line[x + o] + line[x - o])
                total = ca * total
                if cb != 0.0:
                    total = total + cb * line[x]
                if cg != 0.0:
                    total = total + cg * fld[prev, 3 + x, rows, :]
                fld[nxt, 3 + x, rows, :] = total
                here = after
            return carry

        lax.fori_loop(0, 6, along_x, 0, unroll=3)

        def outer(a, carry):
            xs = jnp.minimum(x_ref[a] >> 1, 26)
            z0 = z_ref[a]
            win = (nxt, pl.ds(3 + xs, 6), pl.ds(8 + z0, 16), slice(None))
            weight = scaled[pl.ds(a, 1), :] * (strength_ref[a] * (ca / PROJ_CELLS))
            fld[win] = fld[win] + weight[None] * tiles[pl.ds(6 * a, 6)]
            return carry

        lax.fori_loop(0, 64, outer, 0, unroll=4)

    def send(which, place):
        for i in range(32):
            zb, q = i // 4, i % 4
            for j in range(4):
                xp = 8 * q + 4 * core + j
                for kh in range(2):
                    z = 8 + 6 * zb + 3 * kh
                    to = ((2 * j + kh) * 32 + i) * 6 + place
                    out_ref[to : to + 3, :] = fld[which, 3 + xp, z : z + 3, :]

    step(0, 1, 2, 1.0 / HALF, -CENTER / HALF, 0.0)
    step(1, 2, 0, 2.0 / HALF, -2.0 * CENTER / HALF, -1.0)
    step(2, 0, 1, 2.0 / HALF, -2.0 * CENTER / HALF, -1.0)
    step(0, 1, 2, 2.0 / HALF, -2.0 * CENTER / HALF, -1.0)
    step(1, 2, 0, 1.0, 0.0, 0.0)
    send(1, 0)
    send(2, 3)


def band_matrix(n, blocks):
    taps = np.zeros((n * blocks, n * blocks), np.float32)
    for b in range(blocks):
        for k in range(n):
            for o in range(1, 7):
                for to in (k - o, k + o):
                    if 0 <= to < n:
                        taps[b * n + k, b * n + to] = KIN[o]
    return taps


def box_rows():
    pick = np.zeros((24, 96, 96), np.float32)
    for begin in (0, 2, 4):
        for first in range(8):
            for w in range(6):
                xp = first + w
                for z in range(10):
                    row, slot = divmod(begin + xp % 4 + 4 * z, 6)
                    pick[4 * begin + first, 16 * w + z, 16 * slot + 8 * (xp // 4 % 2) + row] = 1.0
    return pick


def two_parts(taps, axis):
    high = jnp.asarray(taps).astype(jnp.bfloat16)
    rest = (jnp.asarray(taps) - high.astype(F32)).astype(jnp.bfloat16)
    return jnp.concatenate([high, rest], axis=axis)


def same_core():
    return [[2 * i + c for i in range(32)] for c in range(2)]


def same_core_all():
    return [[(2 * i + c) * 8 + y for y in range(8) for i in range(32)] for c in range(2)]


def near_groups():
    return [
        [(16 * z + 2 * x + c) * 8 + 2 * t + u for x in range(8) for u in range(2)]
        for z in range(4)
        for c in range(2)
        for t in range(4)
    ]


def far_groups():
    return [
        [(16 * z + 2 * x + c) * 8 + 2 * t + u for z in range(4) for t in range(4)]
        for x in range(8)
        for c in range(2)
        for u in range(2)
    ]


def exchange(values, groups):
    return lax.all_to_all(values, ("dom", "band"), 0, 0, tiled=True, axis_index_groups=groups)


def pack(at, proj, pot):
    return pl.pallas_call(
        pack_kernel,
        out_shape=jax.ShapeDtypeStruct((32, P1_ROWS, 128), F32),
        in_specs=[smem()] * 3 + [vmem()] * 2,
        out_specs=vmem(),
        scratch_shapes=[pltpu.VMEM((64, 48, 128), F32)],
        compiler_params=params(56),
        name="pack",
    )(*at, proj, pot)


def boxes(at, got, orb):
    return pl.pallas_call(
        boxes_kernel,
        out_shape=jax.ShapeDtypeStruct((32, P2_ROWS, 128), F32),
        in_specs=[smem()] + [vmem()] * 2,
        out_specs=vmem(),
        scratch_shapes=[pltpu.VMEM((2, 40, 128), F32)],
        compiler_params=params(56),
        name="boxes",
    )(at[0], got, orb)


def chebyshev(at, strength, own, oth, own_pot, oth_pot):
    tapy = two_parts(band_matrix(NY, 2), 1)
    tapz = two_parts(band_matrix(48, 1), 0)
    return pl.pallas_call(
        filter_kernel,
        out_shape=jax.ShapeDtypeStruct((1536, 128), F32),
        in_specs=[smem()] * 4 + [vmem()] * 7,
        out_specs=vmem(),
        scratch_shapes=[
            pltpu.VMEM((3, 38, 64, 128), F32),
            pltpu.VMEM((32, 48, 128), F32),
            pltpu.VMEM((64, 16, 128), F32),
            pltpu.VMEM((64 * 6, 16, 128), F32),
            pltpu.VMEM((64, 128), F32),
            pltpu.VMEM((64, 128), F32),
        ],
        compiler_params=params(24),
        name="chebyshev",
    )(*at, strength, tapy, tapz, jnp.asarray(box_rows(), jnp.bfloat16), own, oth, own_pot, oth_pot)


def dot(a, b):
    return jnp.dot(a, b, precision=HIGH, preferred_element_type=F32)


def dot_t(a, b):
    return lax.dot_general(a, b, (((1,), (1,)), ((), ())), precision=HIGH, preferred_element_type=F32)


def parts_of(a):
    high = a.astype(jnp.bfloat16)
    return high, (a - high.astype(F32)).astype(jnp.bfloat16)


def dot_parts(a, b, turn=False):
    dims = (((1,), (1 if turn else 0,)), ((), ()))
    (ah, ar), (bh, br) = a, b
    total = lax.dot_general(ah, br, dims, preferred_element_type=F32)
    total = total + lax.dot_general(ar, bh, dims, preferred_element_type=F32)
    return total + lax.dot_general(ah, bh, dims, preferred_element_type=F32)


def gram_kernel(both_ref, mine_ref, other_ref, f_ref):
    core = place()[0] & 1
    f = [both_ref[pl.ds(r, 256, stride=6), :] for r in range(3)]
    for r in range(3):
        f_ref[r] = f[r]
    f = jnp.concatenate(f, axis=1)
    g = jnp.concatenate([both_ref[pl.ds(3 + r, 256, stride=6), :] for r in range(3)], axis=1)
    f = parts_of(f)
    corr = dot_parts(f, f, True)
    ham = dot_parts(f, parts_of(g), True)
    row = lax.broadcasted_iota(jnp.int32, (256, 256), 0)
    col = lax.broadcasted_iota(jnp.int32, (256, 256), 1)
    packed = jnp.where(row >= col, corr, ham)
    diag = jnp.sum(jnp.where(row == col, ham, 0.0), axis=0, keepdims=True)
    for ref, first in ((mine_ref, core == 0), (other_ref, core == 1)):
        half = jnp.where(first, packed[:, 0:128], packed[:, 128:256])
        for q in range(16):
            ref[q, 0:16, :] = half[16 * q : 16 * q + 16]
            ref[q, 16:24, :] = jnp.zeros((8, 128), F32)
        ref[0, 16:17, :] = jnp.where(first, diag[:, 0:128], diag[:, 128:256])


def ortho_kernel(own_ref, oth_ref, every_ref, rot_ref, proj_ref, corr, ham, inv, work, every, arrived):
    fetch = pltpu.make_async_copy(every_ref, every, arrived)
    fetch.start()
    me, block = place()
    core = me & 1
    row = lax.broadcasted_iota(jnp.int32, (256, 256), 0)
    col = lax.broadcasted_iota(jnp.int32, (256, 256), 1)
    below = row > col
    same = row == col
    scale = 1.0 / NCELLS
    diag = []
    for h in range(2):
        for q in range(16):
            half = jnp.where(core == h, own_ref[q, 0:16, :], oth_ref[q, 0:16, :])
            work[16 * q : 16 * q + 16, 128 * h : 128 * h + 128] = half
        diag.append(jnp.where(core == h, own_ref[0, 16:17, :], oth_ref[0, 16:17, :]))
    packed = work[...] * scale
    turned = packed.T
    diag = jnp.concatenate(diag, axis=1) * scale
    corr[...] = jnp.where(row >= col, packed, turned)
    ham[...] = jnp.where(same, diag, jnp.where(below, turned, packed))

    def half_lower(e):
        return jnp.where(below, e, jnp.where(same, 0.5 * e, 0.0))

    own = jnp.where(same, corr[...], 0.0)
    by_col = lax.rsqrt(jnp.sum(own, axis=0, keepdims=True))
    by_row = lax.rsqrt(jnp.sum(own, axis=1, keepdims=True))
    first = half_lower(by_row * corr[...] * by_col - jnp.where(same, 1.0, 0.0))
    inv[...] = jnp.where(same, by_col, 0.0) - first * by_col

    def rough(a, b, turn=False):
        dims = (((1,), (1 if turn else 0,)), ((), ()))
        return lax.dot_general(
            a.astype(jnp.bfloat16), b.astype(jnp.bfloat16), dims, preferred_element_type=F32
        )

    for _ in range(2):
        x = inv[...]
        e = rough(rough(x, corr[...]), x, True) - jnp.where(same, 1.0, 0.0)
        inv[...] = x - rough(half_lower(e), x)

    def refine(state):
        count, _ = state
        x = inv[...]
        e = dot_t(dot(x, corr[...]), x) - jnp.where(same, 1.0, 0.0)
        inv[...] = x - dot(half_lower(e), x)
        return count + 1, jnp.sum(e * e)

    def going(state):
        count, size = state
        return (count < 8) & jnp.logical_not(size < 1e-6)

    _, size = lax.while_loop(going, refine, (jnp.int32(0), jnp.float32(1.0)))
    least = jnp.min(jnp.where(same, inv[...], 1.0))

    @pl.when(jnp.logical_not((size < 1e-6) & (least > 0.0)))
    def _():
        work[...] = corr[...]
        inv[...] = jnp.where(same, 1.0, 0.0)

        def column(j, carry):
            picked = jnp.sum(jnp.where(col == j, work[...], 0.0), axis=1, keepdims=True)
            at_j = lax.broadcasted_iota(jnp.int32, (256, 1), 0)
            pivot = jnp.sum(jnp.where(at_j == j, picked, 0.0), axis=0, keepdims=True)
            factor = 1.0 / jnp.sqrt(pivot)
            inv[pl.ds(j, 1), :] = inv[pl.ds(j, 1), :] * factor
            down = jnp.where(at_j > j, picked, 0.0) * factor
            work[...] = work[...] - down * (work[pl.ds(j, 1), :] * factor)
            inv[...] = inv[...] - down * inv[pl.ds(j, 1), :]
            return carry

        lax.fori_loop(0, 256, column, 0)

    x = inv[...]
    mine = inv[pl.ds(pl.multiple_of(32 * block, 32), 32), :]
    proj_ref[...] = dot_t(dot(mine, ham[...]), x)
    rows = parts_of(mine)
    fetch.wait()
    for part in range(8):
        j, kh = part // 2, part % 2
        f = jnp.concatenate([every[3 * part + t] for t in range(3)], axis=1)
        turned = dot_parts(rows, parts_of(f))
        for t in range(3):
            rot_ref[pl.ds((3 * kh + t) * 4 + j, 32, stride=24), :] = turned[:, 128 * t : 128 * t + 128]


def gram(both):
    return pl.pallas_call(
        gram_kernel,
        out_shape=[jax.ShapeDtypeStruct((16, 24, 128), F32)] * 2 + [jax.ShapeDtypeStruct((3, 256, 128), F32)],
        in_specs=[vmem()],
        out_specs=[vmem()] * 3,
        compiler_params=params(8),
        name="gram",
    )(both)


def ortho(own, oth, every):
    return pl.pallas_call(
        ortho_kernel,
        out_shape=[jax.ShapeDtypeStruct((768, 128), F32), jax.ShapeDtypeStruct((32, 256), F32)],
        in_specs=[vmem(), vmem(), pl.BlockSpec(memory_space=pl.ANY)],
        out_specs=[vmem()] * 2,
        scratch_shapes=[pltpu.VMEM((256, 256), F32)] * 4
        + [pltpu.VMEM((24, 256, 128), F32), pltpu.SemaphoreType.DMA(())],
        compiler_params=params(56),
        name="ortho",
    )(own, oth, every)


def swap_cores(values):
    return lax.ppermute(values, "dom", [(i, i ^ 1) for i in range(64)])


def sum_everywhere(values):
    for groups in (near_groups(), far_groups()):
        part = jnp.sum(exchange(values, groups), axis=0)
        values = jnp.broadcast_to(part[None], values.shape)
    return exchange(values, near_groups())


def on_device(orbitals, potential, proj_shape, proj_strength, atom_z, atom_x, atom_y):
    at = (atom_z, atom_x, atom_y)
    first = pack(at, proj_shape.reshape(64, 24, 128), potential.reshape(24, 128))
    first = lax.all_to_all(first, "dom", 0, 0, tiled=True, axis_index_groups=same_core())
    first_oth = swap_cores(first)
    second = boxes(at, first, orbitals.reshape(32, 24, 128))
    second = lax.all_to_all(second, "dom", 0, 0, tiled=True, axis_index_groups=same_core())
    second_oth = swap_cores(second)
    both = chebyshev(at, proj_strength, second, second_oth, first, first_oth)
    both = both.reshape(256, 3, 2, 128)
    both = exchange(both, same_core_all())
    both = both.reshape(1536, 128)
    mine, other, filtered = gram(both)
    every = lax.all_gather(filtered, "band", axis=0, tiled=True)
    mine = sum_everywhere(mine + swap_cores(other))
    rotated, projected = ortho(mine, swap_cores(mine), every)
    return (rotated.reshape(32, 1, 6, 512), projected)


def solution(mesh):
    return jax.shard_map(
        on_device,
        mesh=mesh,
        in_specs=(
            P("band", "dom", None, None),
            P("dom", None, None),
            P(None, "dom", None, None),
            P(),
            P(),
            P(),
            P(),
        ),
        out_specs=(P("band", "dom", None, None), P("band", None)),
        check_vma=False,
    )
```
